32 devices in a mesh: region: 4 (over z), block: 8 (over y, x, core).
Axes of the slice: x: 2, y: 2, z: 4, core: 2. Of those that a mesh axis runs over, the one named last changes fastest.
Arguments:
- features: bfloat16 [128, 64, 512], P(('region', 'block')), may hold values from -6 to 6
- counts: int32 [128], P(('region', 'block')), may hold values from 0 to 512, as said below
- rebalance: int32 [128], P(('region', 'block')), may hold values from -1 to 63, as said below
- neighbors: int32 [128, 26], P(('region', 'block')), may hold values from -1 to 127, as said below
- coarse_owner: int32 [128], P(('region', 'block')), may hold values from -1 to 3, as said below
- conv_weight: bfloat16 [27, 64, 128], replicated, may hold values from -0.15625 to 0.15625
- convolution_bias_vector: float32 [128], replicated, may hold values from -3 to 3
- merged_adjoint: bfloat16 [64, 8192], P(('region', 'block')), may hold values from -0.119628906 to 0.119628906
Outputs:
- pooled: bfloat16 [64, 8192], P(('region', 'block'))
- weight_grad: float32 [27, 64, 128], replicated
- bias_grad: float32 [128], replicated
The draws below stay inside these ranges and needn't reach their ends.
Inputs may be any that keep to these rules, and one draw needn't show every extreme that they name: `counts`: 0 marks an empty block; exactly half of each region group's blocks are occupied. `rebalance`: -1 for an empty block; else a row of the block's own region group, each row of a group taken by exactly one block; of the blocks of one device at most 1 have rows on one same device. `neighbors`: -1 where an offset has no occupied neighbour and at every offset of an empty block; neighbours at offsets with ea = 0 lie on the same device, the others on the same device or one of the two beside it along block in the same region group. `coarse_owner`: -1 for an empty block; of the blocks on one device of the working layout at most 1 have the same coarse owner.
All inputs are finite; a program needn't handle non-finite values.
Results may differ from the reference program's by a relative error of at most 0.0029.
Values may be sent and summed in bfloat16 or wider, within the bound.
A program may use at most 128 MiB of HBM per device.

```python
import math
import jax
import jax.numpy as jnp
from jax import lax

C_IN = 64
C_OUT = 128
TAPS = 27
HOME = 4
WORK = 2
BLOCKS = 128
ROWS = 64
N_REGION = 4
N_BLOCK = 8


def layout(key):
    region_count = N_REGION
    device_count = N_BLOCK
    home_slots = HOME
    work_slots = HOME // 2
    group_slots = device_count * home_slots
    subkeys = jax.random.split(key, 7)
    crowded_device = jax.random.randint(subkeys[0], (region_count, 1), 0, device_count)
    device_weight = jax.random.randint(subkeys[1], (region_count, device_count), 1, 5)
    random_noise = jax.random.randint(subkeys[2], (region_count, device_count, home_slots), 0, 1024)
    scores = random_noise * device_weight[:, :, None]
    device_ids = jnp.arange(device_count, dtype=jnp.int32)[None, :, None]
    scores = jnp.where(device_ids == crowded_device[:, :, None], 5000, scores)
    scores = scores.reshape(region_count, group_slots) * group_slots + jnp.arange(group_slots, dtype=jnp.int32)[None, :]
    chosen = jax.lax.top_k(scores, device_count * work_slots)[1]
    group_ids = jnp.arange(region_count, dtype=jnp.int32)[:, None]
    occupied = jnp.zeros((region_count, group_slots), jnp.int32).at[group_ids, chosen].set(1)
    ranking = jnp.maximum(jnp.cumsum(occupied, axis=1) - 1, 0)
    shuffles = jax.vmap(lambda subkey: jax.random.permutation(subkey, device_count))(jax.random.split(subkeys[3], region_count))
    dest_device = jnp.take_along_axis(shuffles, ranking % device_count, axis=1)
    dest_slot = ranking // device_count
    rebalance = jnp.where(occupied == 1, (group_ids * device_count + dest_device) * work_slots + dest_slot, -1)
    raw_counts = jnp.minimum(jax.random.randint(subkeys[4], (region_count, group_slots), 1, 700), 512)
    counts = jnp.where(occupied == 1, raw_counts, 0)
    position_of = jax.vmap(lambda subkey: jax.random.permutation(subkey, home_slots))(jax.random.split(subkeys[5], region_count * device_count)).reshape(region_count, device_count, home_slots)
    slot_of = jnp.argsort(position_of, axis=2)
    x_layers = home_slots // 4
    x_local = position_of // 4
    y_coord = position_of // 2 % 2
    z_coord = position_of % 2
    x_global = device_ids * x_layers + x_local
    occupied_cube = occupied.reshape(region_count, device_count, home_slots)
    group_cube = jnp.arange(region_count, dtype=jnp.int32)[:, None, None]
    entries = []
    for delta_x in (-1, 0, 1):
        for delta_y in (-1, 0, 1):
            for delta_z in (-1, 0, 1):
                if delta_x == 0 and delta_y == 0 and (delta_z == 0):
                    continue
                next_x = x_global + delta_x
                next_y = y_coord + delta_y
                next_z = z_coord + delta_z
                within = (next_x >= 0) & (next_x < device_count * x_layers) & (next_y >= 0) & (next_y < 2) & (next_z >= 0) & (next_z < 2)
                clipped_x = jnp.clip(next_x, 0, device_count * x_layers - 1)
                next_device = clipped_x // x_layers
                next_position = clipped_x % x_layers * 4 + jnp.clip(next_y, 0, 1) * 2 + jnp.clip(next_z, 0, 1)
                next_slot = slot_of[group_cube, next_device, next_position]
                usable = within & (occupied_cube == 1) & (occupied_cube[group_cube, next_device, next_slot] == 1)
                global_index = (group_cube * device_count + next_device) * home_slots + next_slot
                entries.append(jnp.where(usable, global_index, -1))
    neighbors = jnp.stack(entries, axis=-1).reshape(region_count * group_slots, 26)
    twisting = jax.vmap(lambda subkey: jax.random.permutation(subkey, region_count))(jax.random.split(subkeys[6], device_count))
    coarse = jnp.where(occupied == 1, (group_ids + twisting[dest_device, dest_slot % region_count]) % region_count, -1)
    return (counts.reshape(-1).astype(jnp.int32), rebalance.reshape(-1).astype(jnp.int32), neighbors.astype(jnp.int32), coarse.reshape(-1).astype(jnp.int32))


def draw_counts(key, part):
    return layout(key)[0]


def draw_rebalance(key, part):
    return layout(key)[1]


def draw_neighbors(key, part):
    return layout(key)[2]


def draw_coarse_owner(key, part):
    return layout(key)[3]


def level_of(stream_key, shape, shards, low, high):
    def one(axis_at, shards_of):
        draws = jax.random.uniform(jax.random.fold_in(jax.random.fold_in(stream_key, 6), axis_at), (shards_of,), jnp.float32, low / len(shards), high / len(shards))
        return jnp.repeat(jnp.exp(draws), shape[axis_at] // shards_of).reshape((-1,) + (1,) * (len(shape) - axis_at - 1))

    gain = one(*shards[0])
    for cut in shards[1:]:
        gain = gain * one(*cut)
    return gain


def gaussian(key, shape, width, bound, shards=(), kind=jnp.bfloat16):
    loudness = level_of(key, shape, shards, -0.22, 0.18) if shards else 1.0
    result = jax.random.normal(key, shape, jnp.float32) * width * loudness
    return jnp.minimum(jnp.maximum(result, -bound), bound).astype(kind)


def setup_inputs(seed: int = 0) -> dict:
    seeds = jax.random.split(jax.random.key(seed), 9)
    return {
        "features": gaussian(seeds[0], (BLOCKS, C_IN, 512), 1.0, 6.0, ((0, 32),)),
        "counts": draw_counts(jax.random.fold_in(seeds[8], 71), 0),
        "rebalance": draw_rebalance(jax.random.fold_in(seeds[8], 71), 0),
        "neighbors": draw_neighbors(jax.random.fold_in(seeds[8], 71), 0),
        "coarse_owner": draw_coarse_owner(jax.random.fold_in(seeds[8], 71), 0),
        "conv_weight": gaussian(seeds[5], (TAPS, C_IN, C_OUT), (TAPS * C_IN) ** -0.5, 0.15625),
        "convolution_bias_vector": gaussian(seeds[6], (C_OUT,), 0.5, 3.0, (), jnp.float32),
        "merged_adjoint": gaussian(seeds[7], (ROWS, C_OUT * 64), 0.02, 0.119628906, ((0, 32),)),
    }


def filled_fraction(block_counts):
    hashed = (jnp.arange(512, dtype=jnp.int32) * 167) % 512
    return hashed[None, :] < block_counts[:, None]


def offset_list():
    return [(ea, eb, ec) for ea in (-1, 0, 1) for eb in (-1, 0, 1) for ec in (-1, 0, 1) if (ea, eb, ec) != (0, 0, 0)]


def source_range(step):
    return (7, 8) if step < 0 else ((0, 1) if step > 0 else (0, 8))


def target_range(step):
    return (0, 1) if step < 0 else ((9, 10) if step > 0 else (1, 9))


def source_piece(cube_view, offset):
    rows_now, channels = cube_view.shape[0], cube_view.shape[1]
    a_low, a_high = source_range(offset[0])
    b_low, b_high = source_range(offset[1])
    c_low, c_high = source_range(offset[2])
    piece = cube_view[:, :, a_low:a_high, b_low:b_high, c_low:c_high]
    return piece.reshape(rows_now, channels, -1)


def padded_cube(blocks_in, shell_in):
    rows_now, channels = blocks_in.shape[0], blocks_in.shape[1]
    cube = jnp.zeros((rows_now, channels, 10, 10, 10), blocks_in.dtype)
    cube = cube.at[:, :, 1:9, 1:9, 1:9].set(blocks_in.reshape(rows_now, channels, 8, 8, 8))
    pointer = 0
    for offset in offset_list():
        a_low, a_high = target_range(offset[0])
        b_low, b_high = target_range(offset[1])
        c_low, c_high = target_range(offset[2])
        extent = (a_high - a_low) * (b_high - b_low) * (c_high - c_low)
        piece = shell_in[:, :, pointer:pointer + extent].reshape(rows_now, channels, a_high - a_low, b_high - b_low, c_high - c_low)
        cube = cube.at[:, :, a_low:a_high, b_low:b_high, c_low:c_high].set(piece)
        pointer = pointer + extent
    return cube


def taps(blocks_in, shell_in):
    rows_now, channels = blocks_in.shape[0], blocks_in.shape[1]
    cube = padded_cube(blocks_in, shell_in)
    pieces = []
    for ea in (-1, 0, 1):
        for eb in (-1, 0, 1):
            for ec in (-1, 0, 1):
                window = cube[:, :, 1 + ea:9 + ea, 1 + eb:9 + eb, 1 + ec:9 + ec]
                pieces.append(window.reshape(rows_now, channels, 512))
    return jnp.concatenate(pieces, axis=1)


def pool_table():
    voxels = jnp.arange(512, dtype=jnp.int32)
    cell_index = ((voxels // 128) * 4 + (voxels // 16) % 4) * 4 + (voxels % 8) // 2
    return jnp.where(cell_index[:, None] == jnp.arange(64, dtype=jnp.int32)[None, :], 0.125, 0.0).astype(jnp.float32)


def reference(features, counts, rebalance, neighbors, coarse_owner, conv_weight, convolution_bias_vector, merged_adjoint):
    block_total = features.shape[0]
    channels = features.shape[1]
    result_feature_count = convolution_bias_vector.shape[0]
    tap_count = conv_weight.shape[0]
    row_total = block_total // 2
    occupied_mask = filled_fraction(counts)
    masked = jnp.where(occupied_mask[:, None, :], features, jnp.zeros_like(features))
    masked_cube = masked.reshape(block_total, channels, 8, 8, 8)
    present = neighbors >= 0
    safe_index = jnp.where(present, neighbors, 0)
    shell_parts = []
    for column, offset in enumerate(offset_list()):
        piece = jnp.take(source_piece(masked_cube, offset), safe_index[:, column], axis=0)
        shell_parts.append(jnp.where(present[:, column][:, None, None], piece, jnp.zeros_like(piece)))
    shells = jnp.concatenate(shell_parts, axis=2)
    source = jnp.zeros((row_total,), jnp.int32).at[jnp.where(rebalance >= 0, rebalance, row_total)].set(
        jnp.arange(block_total, dtype=jnp.int32), mode="drop")
    row_ids = jnp.arange(row_total, dtype=jnp.int32)
    owner_device = (row_ids // WORK) % N_BLOCK
    owner_slot = row_ids % WORK
    receiving_line = (jnp.take(coarse_owner, source) * N_BLOCK + owner_device) * WORK + owner_slot
    flattened_weight = conv_weight.reshape(tap_count * channels, result_feature_count).astype(jnp.float32)
    table = pool_table()
    sample_number = math.gcd(row_total, 32)

    def forward(lookup):
        stacked_layers = taps(masked[lookup], shells[lookup])
        before_activation = jnp.einsum("esh,sb->ebh", stacked_layers.astype(jnp.float32), flattened_weight) + convolution_bias_vector[None, :, None]
        activation = jnp.where(filled_fraction(counts[lookup])[:, None, :], jax.nn.silu(before_activation), 0.0)
        pooled_part = jnp.einsum("ncv,vp->ncp", activation, table, precision=lax.Precision.HIGHEST)
        return pooled_part.reshape(sample_number, result_feature_count * 64).astype(jnp.bfloat16)

    pooled_work = lax.map(forward, source.reshape(-1, sample_number)).reshape(row_total, result_feature_count * 64)
    pooled = jnp.zeros_like(pooled_work).at[receiving_line].set(pooled_work)
    derivative_of_evened_tiles = jnp.take(merged_adjoint, receiving_line, axis=0)

    def backward(running, component):
        lookup, part_grad = component
        stacked_layers = taps(masked[lookup], shells[lookup])
        before_activation = jnp.einsum("esh,sb->ebh", stacked_layers.astype(jnp.float32), flattened_weight) + convolution_bias_vector[None, :, None]
        mask_view = filled_fraction(counts[lookup])[:, None, :]
        spread_grad = jnp.einsum("ncp,vp->ncv", part_grad.reshape(sample_number, result_feature_count, 64).astype(jnp.float32),
                                 table, precision=lax.Precision.HIGHEST)
        sigmoid_value = jax.nn.sigmoid(before_activation)
        grad_pre = jnp.where(mask_view, spread_grad * sigmoid_value * (1.0 + before_activation * (1.0 - sigmoid_value)), 0.0)
        gradient_lower_bits = grad_pre.astype(jnp.bfloat16)
        partial_weight = jnp.einsum("sez,stz->et", stacked_layers.astype(jnp.float32), gradient_lower_bits.astype(jnp.float32))
        return (running[0] + partial_weight, running[1] + jnp.sum(grad_pre, axis=(0, 2))), None

    start_state = (jnp.zeros((tap_count * channels, result_feature_count), jnp.float32), jnp.zeros((result_feature_count,), jnp.float32))
    totals, _ = lax.scan(backward, start_state, (source.reshape(-1, sample_number),
                                                 derivative_of_evened_tiles.reshape(-1, sample_number, result_feature_count * 64)))
    return pooled, totals[0].reshape(tap_count, channels, result_feature_count), totals[1]
```

```python
import functools
import math

import jax
import jax.numpy as jnp
from jax import lax
from jax.experimental import pallas as pl
from jax.experimental.pallas import tpu as pltpu
from jax.sharding import PartitionSpec as P

MESH = pl.DeviceIdType.MESH
VMEM_LIMIT = 48 * 1024 * 1024
F32 = jnp.float32
BF16 = jnp.bfloat16


def greet(region, block, regions, blocks):
    barrier = pltpu.get_barrier_semaphore()
    for k in range(1, blocks):
        pl.semaphore_signal(
            barrier, inc=1, device_id=(region, lax.rem(block + k, blocks)), device_id_type=MESH
        )
    for k in range(1, regions):
        pl.semaphore_signal(
            barrier, inc=1, device_id=(lax.rem(region + k, regions), block), device_id_type=MESH
        )
    pl.semaphore_wait(barrier, blocks + regions - 2)


def remote(src, dst, send_sem, recv_sem, device):
    return pltpu.make_async_remote_copy(
        src_ref=src,
        dst_ref=dst,
        send_sem=send_sem,
        recv_sem=recv_sem,
        device_id=device,
        device_id_type=MESH,
    )


def exchange_kernel(
    regions,
    blocks,
    counts_ref,
    rebalance_ref,
    owner_ref,
    features_ref,
    adjoint_ref,
    layers_ref,
    cotangent_ref,
    tags_ref,
    adjoints,
    outgoing,
    adj_send,
    adj_recv,
    tag_send,
    tag_recv,
    lay_send,
    lay_recv,
    cot_send,
    cot_recv,
):
    region, block = lax.axis_index("region"), lax.axis_index("block")
    home = features_ref.shape[0]
    work = adjoint_ref.shape[0]
    rows = lax.broadcasted_iota(jnp.int32, (blocks, 128), 0)
    codes = jnp.full((blocks, 128), -1, jnp.int32)
    for h in range(home):
        line = rebalance_ref[h]
        device = jnp.where(line >= 0, lax.rem(lax.div(line, work), blocks), -1)
        code = owner_ref[h] * work + lax.rem(line, work)
        codes = jnp.where(rows == device, code, codes)
    tags_ref[block] = codes
    lanes = lax.broadcasted_iota(jnp.int32, (1, 64), 1)
    for h in range(home):
        for side, start in enumerate((0, 448)):
            live = (((lanes + start) * 167) & 511) < counts_ref[h]
            values = features_ref[h, :, start : start + 64].astype(F32)
            layers_ref[1, h, :, side * 64 : side * 64 + 64] = jnp.where(live, values, 0.0).astype(
                BF16
            )
    adjoints[region] = adjoint_ref[...]
    greet(region, block, regions, blocks)

    before = lax.rem(block + blocks - 1, blocks)
    after = lax.rem(block + 1, blocks)
    sends = []
    for k in range(1, regions):
        copy = remote(
            adjoints.at[region],
            adjoints.at[region],
            adj_send.at[k],
            adj_recv.at[k],
            (lax.rem(region + k, regions), block),
        )
        copy.start()
        sends.append(copy)
    for k in range(1, blocks):
        copy = remote(
            tags_ref.at[block],
            tags_ref.at[block],
            tag_send.at[k],
            tag_recv.at[k],
            (region, lax.rem(block + k, blocks)),
        )
        copy.start()
        sends.append(copy)
    for i, (slot, target) in enumerate(((2, before), (0, after))):
        copy = remote(
            layers_ref.at[1], layers_ref.at[slot], lay_send.at[i], lay_recv.at[i], (region, target)
        )
        copy.start()
        sends.append(copy)
    for k in range(1, regions):
        source = lax.rem(region + regions - k, regions)
        remote(
            adjoints.at[source],
            adjoints.at[source],
            adj_send.at[k],
            adj_recv.at[k],
            (source, block),
        ).wait_recv()
    for k in range(1, blocks):
        source = lax.rem(block + blocks - k, blocks)
        remote(
            tags_ref.at[source],
            tags_ref.at[source],
            tag_send.at[k],
            tag_recv.at[k],
            (region, source),
        ).wait_recv()
        code = tags_ref[source, pl.ds(block, 1), :64]

        def add(j, total, code=code):
            chosen = jnp.where(code == j, 1.0, 0.0)
            return total + chosen * adjoints[lax.div(j, work), lax.rem(j, work)].astype(F32)

        total = lax.fori_loop(
            0, regions * work, add, jnp.zeros(cotangent_ref.shape[1:], F32)
        )
        outgoing[source] = total.astype(BF16)
        copy = remote(
            outgoing.at[source],
            cotangent_ref.at[block],
            cot_send.at[blocks - k],
            cot_recv.at[blocks - k],
            (region, source),
        )
        copy.start()
        sends.append(copy)
    code = tags_ref[block, pl.ds(block, 1), :64]

    def add_own(j, total):
        chosen = jnp.where(code == j, 1.0, 0.0)
        return total + chosen * adjoints[lax.div(j, work), lax.rem(j, work)].astype(F32)

    cotangent_ref[block] = lax.fori_loop(
        0, regions * work, add_own, jnp.zeros(cotangent_ref.shape[1:], F32)
    ).astype(BF16)
    for i, (slot, target) in enumerate(((2, after), (0, before))):
        remote(
            layers_ref.at[1], layers_ref.at[slot], lay_send.at[i], lay_recv.at[i], (region, target)
        ).wait_recv()
    for k in range(1, blocks):
        source = lax.rem(block + blocks - k, blocks)
        remote(
            outgoing.at[source],
            cotangent_ref.at[source],
            cot_send.at[k],
            cot_recv.at[k],
            (region, source),
        ).wait_recv()
    for copy in sends:
        copy.wait_send()


def column(ea, eb, ec):
    t = 9 * (ea + 1) + 3 * (eb + 1) + (ec + 1)
    return t if t < 13 else t - 1


def compute_kernel(
    blocks,
    counts_ref,
    rebalance_ref,
    neighbors_ref,
    features_ref,
    layers_ref,
    cotangent_ref,
    weight_ref,
    bias_ref,
    pooled_ref,
    grad_ref,
    bias_grad_ref,
    cubes,
    slabs,
    stacked,
    total,
):
    home, channels = features_ref.shape[0], features_ref.shape[1]
    work = home // 2
    first = (lax.axis_index("region") * blocks + lax.axis_index("block")) * home
    voxel = lax.broadcasted_iota(jnp.int32, (1, 512), 1)
    hashed = (voxel * 167) & 511
    for h in range(home):
        cubes[h] = jnp.where(hashed < counts_ref[h], features_ref[h].astype(F32), 0.0)
        for d in range(3):
            slabs[d * home + h] = layers_ref[d, h].astype(F32)
    cubes[home] = jnp.zeros(cubes.shape[1:], F32)
    slabs[3 * home] = jnp.zeros(slabs.shape[1:], F32)
    total[...] = jnp.zeros_like(total)
    bias_grad_ref[...] = jnp.zeros_like(bias_grad_ref)
    pooled_ref[...] = jnp.zeros_like(pooled_ref)

    v = lax.broadcasted_iota(jnp.int32, (512, 64), 0)
    cell = ((v >> 7) * 4 + ((v >> 4) & 3)) * 4 + ((v & 7) >> 1)
    table = jnp.where(
        cell == lax.broadcasted_iota(jnp.int32, (512, 64), 1), 0.125, 0.0
    ).astype(BF16)
    lane = lax.broadcasted_iota(jnp.int32, (1, 640), 1)
    b_at, c_at = (lane >> 3) & 7, lane & 7
    half = lax.broadcasted_iota(jnp.int32, (1, 128), 1) < 64

    def shifted(x, offset):
        return pltpu.roll(x, (-offset) % 640, 1)

    def one_block(g, carry):
        def slab(ea, fb, fc):
            target = neighbors_ref[g, column(ea, fb, fc)]
            return slabs[jnp.where(target >= 0, target - (first - home), 3 * home)]

        def extended(fb, fc):
            if (fb, fc) == (0, 0):
                middle = cubes[g]
            else:
                target = neighbors_ref[g, column(0, fb, fc)]
                middle = cubes[jnp.where(target >= 0, target - first, home)]
            ends = jnp.where(half, slab(1, fb, fc), slab(-1, fb, fc))
            return jnp.concatenate([middle, ends], axis=1)

        for ec in (-1, 0, 1):
            along = {}
            for fb in (-1, 0, 1):
                if ec == 0:
                    along[fb] = extended(fb, 0)
                else:
                    out = (c_at + ec) != ((c_at + ec) & 7)
                    along[fb] = jnp.where(
                        out,
                        shifted(extended(fb, ec), -7 * ec),
                        shifted(extended(fb, 0), ec),
                    )
            for eb in (-1, 0, 1):
                if eb == 0:
                    plane = along[0]
                else:
                    out = (b_at + eb) != ((b_at + eb) & 7)
                    plane = jnp.where(
                        out, shifted(along[eb], -56 * eb), shifted(along[0], 8 * eb)
                    )
                for ea in (-1, 0, 1):
                    tap = 9 * (ea + 1) + 3 * (eb + 1) + (ec + 1)
                    moved = plane if ea == 0 else shifted(plane, 64 * ea)
                    stacked[tap * channels : (tap + 1) * channels, :] = moved[:, :512].astype(BF16)

        preact = (
            lax.dot_general(
                weight_ref[...],
                stacked[...],
                (((0,), (0,)), ((), ())),
                preferred_element_type=F32,
            )
            + bias_ref[...]
        )
        live = hashed < counts_ref[g]
        gate = jax.nn.sigmoid(preact)
        active = jnp.where(live, preact * gate, 0.0)
        high = active.astype(BF16)
        low = (active - high.astype(F32)).astype(BF16)
        pooled = jnp.dot(high, table, preferred_element_type=F32) + jnp.dot(
            low, table, preferred_element_type=F32
        )
        line = rebalance_ref[g]
        device = jnp.where(line >= 0, lax.rem(lax.div(line, work), blocks), blocks)
        pooled_ref[device] = pooled.astype(BF16)
        spread = lax.dot_general(
            cotangent_ref[jnp.minimum(device, blocks - 1)],
            table,
            (((1,), (1,)), ((), ())),
            preferred_element_type=F32,
        )
        grad = jnp.where(live, spread * gate * (1.0 + preact * (1.0 - gate)), 0.0)
        grad_high = grad.astype(BF16)
        grad_low = (grad - grad_high.astype(F32)).astype(BF16)
        total[...] += lax.dot_general(
            stacked[...], grad_high, (((1,), (1,)), ((), ())), preferred_element_type=F32
        )
        ones = jnp.ones((8, 512), BF16)
        for part in (grad_high, grad_low):
            bias_grad_ref[...] += lax.dot_general(
                ones, part, (((1,), (1,)), ((), ())), preferred_element_type=F32
            )
        return carry

    lax.fori_loop(0, home, one_block, 0)
    used = total.shape[0]
    grad_ref[:used, :] = total[...].astype(BF16)
    if grad_ref.shape[0] > used:
        grad_ref[used:, :] = jnp.zeros((grad_ref.shape[0] - used, grad_ref.shape[1]), BF16)


def reduce_kernel(
    regions,
    blocks,
    shard,
    pooled_in,
    tags_ref,
    grad_ref,
    bias_ref,
    pooled_ref,
    weight_out,
    bias_out,
    pooled_got,
    pooled_sel,
    pooled_end,
    grad_got,
    grad_part,
    grad_slice,
    grad_full,
    grad_all,
    bias_got,
    bias_part,
    p_send,
    p_recv,
    q_send,
    q_recv,
    g_send,
    g_recv,
    h_send,
    h_recv,
    d_send,
    d_recv,
    a_send,
    a_recv,
    b_send,
    b_recv,
    c_send,
    c_recv,
):
    region, block = lax.axis_index("region"), lax.axis_index("block")
    work = pooled_ref.shape[0]
    greet(region, block, regions, blocks)
    sends = []

    def start(*args):
        copy = remote(*args)
        copy.start()
        sends.append(copy)

    def across(k):
        return (region, lax.rem(block + k, blocks))

    def along(k):
        return (lax.rem(region + k, regions), block)

    def part(index):
        return pl.ds(pl.multiple_of(index * shard, 16), shard)

    for k in range(1, blocks):
        peer = lax.rem(block + k, blocks)
        start(pooled_in.at[peer], pooled_got.at[k], p_send.at[k], p_recv.at[k], across(k))
        start(bias_ref, bias_got.at[k], b_send.at[k], b_recv.at[k], across(k))
    for k in range(1, blocks):
        peer = lax.rem(block + k, blocks)
        start(grad_ref.at[part(peer)], grad_got.at[k], g_send.at[k], g_recv.at[k], across(k))
    pooled_got[0] = pooled_in[block]
    for k in range(1, blocks):
        remote(
            pooled_in.at[0], pooled_got.at[k], p_send.at[k], p_recv.at[k], across(k)
        ).wait_recv()

    def select(j, carry):
        def add(k, total):
            code = tags_ref[lax.rem(block + blocks - k, blocks), pl.ds(block, 1), :64]
            return total + jnp.where(code == j, 1.0, 0.0) * pooled_got[k].astype(F32)

        total = lax.fori_loop(0, blocks, add, jnp.zeros(pooled_ref.shape[1:], F32))
        pooled_sel[lax.div(j, work), lax.rem(j, work)] = total.astype(BF16)
        return carry

    lax.fori_loop(0, regions * work, select, 0)
    for k in range(1, regions):
        peer = lax.rem(region + k, regions)
        start(pooled_sel.at[peer], pooled_end.at[k], q_send.at[k], q_recv.at[k], along(k))
    bias_sum = bias_ref[...]
    for k in range(1, blocks):
        remote(bias_ref, bias_got.at[k], b_send.at[k], b_recv.at[k], across(k)).wait_recv()
        bias_sum = bias_sum + bias_got[k]
    bias_part[region] = bias_sum
    for k in range(1, regions):
        start(
            bias_part.at[region], bias_part.at[region], c_send.at[k], c_recv.at[k], along(k)
        )

    for k in range(1, blocks):
        remote(
            grad_ref.at[part(0)], grad_got.at[k], g_send.at[k], g_recv.at[k], across(k)
        ).wait_recv()
    grad_sum = grad_ref[part(block), :].astype(F32)
    for k in range(1, blocks):
        grad_sum = grad_sum + grad_got[k].astype(F32)
    grad_part[...] = grad_sum.reshape(grad_part.shape)
    for k in range(1, regions):
        peer = lax.rem(region + k, regions)
        start(grad_part.at[peer], grad_slice.at[k], h_send.at[k], h_recv.at[k], along(k))
    for k in range(1, regions):
        remote(
            grad_part.at[0], grad_slice.at[k], h_send.at[k], h_recv.at[k], along(k)
        ).wait_recv()
    grad_sum = grad_part[region]
    for k in range(1, regions):
        grad_sum = grad_sum + grad_slice[k]
    grad_full[region] = grad_sum
    for k in range(1, regions):
        start(
            grad_full.at[region], grad_full.at[region], d_send.at[k], d_recv.at[k], along(k)
        )
    for k in range(1, regions):
        source = lax.rem(region + regions - k, regions)
        remote(
            grad_full.at[source], grad_full.at[source], d_send.at[k], d_recv.at[k], along(k)
        ).wait_recv()
    grad_sum = grad_full[...].reshape(shard, -1)
    grad_all[block] = grad_sum.astype(BF16)
    for k in range(1, blocks):
        start(grad_all.at[block], grad_all.at[block], a_send.at[k], a_recv.at[k], across(k))

    for k in range(1, regions):
        source = lax.rem(region + regions - k, regions)
        remote(
            bias_part.at[source], bias_part.at[source], c_send.at[k], c_recv.at[k], along(k)
        ).wait_recv()
        remote(
            pooled_sel.at[0], pooled_end.at[k], q_send.at[k], q_recv.at[k], along(k)
        ).wait_recv()
    bias_sum = bias_part[0]
    for r in range(1, regions):
        bias_sum = bias_sum + bias_part[r]
    bias_out[...] = bias_sum
    for s in range(work):
        rows = pooled_sel[region, s].astype(F32)
        for k in range(1, regions):
            rows = rows + pooled_end[k, s].astype(F32)
        pooled_ref[s] = rows.astype(BF16)

    for k in range(1, blocks):
        source = lax.rem(block + blocks - k, blocks)
        remote(
            grad_all.at[source], grad_all.at[source], a_send.at[k], a_recv.at[k], across(k)
        ).wait_recv()
    rows_total = weight_out.shape[0]
    for w in range(blocks):
        low, high = w * shard, min((w + 1) * shard, rows_total)
        if low < high:
            weight_out[low:high, :] = grad_all[w, : high - low, :].astype(F32)
    for copy in sends:
        copy.wait_send()


def per_device(
    features,
    counts,
    rebalance,
    neighbors,
    coarse_owner,
    conv_weight,
    convolution_bias_vector,
    merged_adjoint,
):
    home, channels = features.shape[0], features.shape[1]
    taps, _, outs = conv_weight.shape
    work = home // 2
    regions, blocks = lax.axis_size("region"), lax.axis_size("block")
    cells = merged_adjoint.shape[1] // outs
    rows = taps * channels
    unit = math.lcm(16, 8 * regions)
    shard = -(-rows // (blocks * unit)) * unit
    vmem = pl.BlockSpec(memory_space=pltpu.VMEM)
    smem = pl.BlockSpec(memory_space=pltpu.SMEM)
    dma = pltpu.SemaphoreType.DMA
    shape = jax.ShapeDtypeStruct

    layers, cotangent, tags = pl.pallas_call(
        functools.partial(exchange_kernel, regions, blocks),
        out_shape=(
            shape((3, home, channels, 128), BF16),
            shape((blocks, outs, cells), BF16),
            shape((blocks, blocks, 128), jnp.int32),
        ),
        in_specs=[smem, smem, smem, vmem, vmem],
        out_specs=(vmem, vmem, vmem),
        scratch_shapes=[
            pltpu.VMEM((regions, work, outs, cells), BF16),
            pltpu.VMEM((blocks, outs, cells), BF16),
            dma((regions,)),
            dma((regions,)),
            dma((blocks,)),
            dma((blocks,)),
            dma((2,)),
            dma((2,)),
            dma((blocks,)),
            dma((blocks,)),
        ],
        compiler_params=pltpu.CompilerParams(
            collective_id=0, has_side_effects=True, vmem_limit_bytes=VMEM_LIMIT
        ),
        name="exchange",
    )(counts, rebalance, coarse_owner, features, merged_adjoint.reshape(work, outs, cells))

    pooled_send, grad_send, bias_send = pl.pallas_call(
        functools.partial(compute_kernel, blocks),
        out_shape=(
            shape((blocks + 1, outs, cells), BF16),
            shape((blocks * shard, outs), BF16),
            shape((8, outs), F32),
        ),
        in_specs=[smem, smem, smem, vmem, vmem, vmem, vmem, vmem],
        out_specs=(vmem, vmem, vmem),
        scratch_shapes=[
            pltpu.VMEM((home + 1, channels, 512), F32),
            pltpu.VMEM((3 * home + 1, channels, 128), F32),
            pltpu.VMEM((rows, 512), BF16),
            pltpu.VMEM((rows, outs), F32),
        ],
        compiler_params=pltpu.CompilerParams(vmem_limit_bytes=VMEM_LIMIT),
        name="convolve",
    )(
        counts,
        rebalance,
        neighbors,
        features,
        layers,
        cotangent,
        conv_weight.reshape(rows, outs),
        convolution_bias_vector.reshape(outs, 1),
    )

    pooled, weight_total, bias_total = pl.pallas_call(
        functools.partial(reduce_kernel, regions, blocks, shard),
        out_shape=(
            shape((work, outs, cells), BF16),
            shape((rows, outs), F32),
            shape((8, outs), F32),
        ),
        in_specs=[vmem] * 4,
        out_specs=(vmem, vmem, vmem),
        scratch_shapes=[
            pltpu.VMEM((blocks, outs, cells), BF16),
            pltpu.VMEM((regions, work, outs, cells), BF16),
            pltpu.VMEM((regions, work, outs, cells), BF16),
            pltpu.VMEM((blocks, shard, outs), BF16),
            pltpu.VMEM((regions, shard // regions, outs), F32),
            pltpu.VMEM((regions, shard // regions, outs), F32),
            pltpu.VMEM((regions, shard // regions, outs), F32),
            pltpu.VMEM((blocks, shard, outs), BF16),
            pltpu.VMEM((blocks, 8, outs), F32),
            pltpu.VMEM((regions, 8, outs), F32),
            dma((blocks,)),
            dma((blocks,)),
            dma((regions,)),
            dma((regions,)),
            dma((blocks,)),
            dma((blocks,)),
            dma((regions,)),
            dma((regions,)),
            dma((regions,)),
            dma((regions,)),
            dma((blocks,)),
            dma((blocks,)),
            dma((blocks,)),
            dma((blocks,)),
            dma((regions,)),
            dma((regions,)),
        ],
        compiler_params=pltpu.CompilerParams(
            collective_id=1, has_side_effects=True, vmem_limit_bytes=VMEM_LIMIT
        ),
        name="reduce",
    )(pooled_send, tags, grad_send, bias_send)
    return (
        pooled.reshape(work, outs * cells),
        weight_total.reshape(taps, channels, outs),
        bias_total[0],
    )


def solution(mesh):
    in_specs = (
        P(("region", "block"), None, None),
        P(("region", "block")),
        P(("region", "block")),
        P(("region", "block"), None),
        P(("region", "block")),
        P(),
        P(),
        P(("region", "block"), None),
    )
    out_specs = (P(("region", "block"), None), P(), P())
    return jax.shard_map(
        per_device, mesh=mesh, in_specs=in_specs, out_specs=out_specs, check_vma=False
    )
```

```python
import functools
import math

import jax
import jax.numpy as jnp
from jax import lax
from jax.experimental import pallas as pl
from jax.experimental.pallas import tpu as pltpu
from jax.sharding import PartitionSpec as P

MESH = pl.DeviceIdType.MESH
VMEM_LIMIT = 48 * 1024 * 1024
F32 = jnp.float32
BF16 = jnp.bfloat16


def greet(region, block, regions, blocks):
    barrier = pltpu.get_barrier_semaphore()
    for k in range(1, blocks):
        pl.semaphore_signal(
            barrier, inc=1, device_id=(region, lax.rem(block + k, blocks)), device_id_type=MESH
        )
    for k in range(1, regions):
        pl.semaphore_signal(
            barrier, inc=1, device_id=(lax.rem(region + k, regions), block), device_id_type=MESH
        )
    pl.semaphore_wait(barrier, blocks + regions - 2)


def remote(src, dst, send_sem, recv_sem, device):
    return pltpu.make_async_remote_copy(
        src_ref=src,
        dst_ref=dst,
        send_sem=send_sem,
        recv_sem=recv_sem,
        device_id=device,
        device_id_type=MESH,
    )


def exchange_kernel(
    regions,
    blocks,
    counts_ref,
    rebalance_ref,
    owner_ref,
    features_ref,
    adjoint_ref,
    layers_ref,
    cotangent_ref,
    tags_ref,
    adjoints,
    outgoing,
    adj_send,
    adj_recv,
    tag_send,
    tag_recv,
    lay_send,
    lay_recv,
    cot_send,
    cot_recv,
):
    region, block = lax.axis_index("region"), lax.axis_index("block")
    home = features_ref.shape[0]
    work = adjoint_ref.shape[0]
    rows = lax.broadcasted_iota(jnp.int32, (blocks, 128), 0)
    codes = jnp.full((blocks, 128), -1, jnp.int32)
    for h in range(home):
        line = rebalance_ref[h]
        device = jnp.where(line >= 0, lax.rem(lax.div(line, work), blocks), -1)
        code = owner_ref[h] * work + lax.rem(line, work)
        codes = jnp.where(rows == device, code, codes)
    tags_ref[block] = codes
    lanes = lax.broadcasted_iota(jnp.int32, (1, 64), 1)
    for h in range(home):
        for side, start in enumerate((0, 448)):
            live = (((lanes + start) * 167) & 511) < counts_ref[h]
            values = features_ref[h, :, start : start + 64].astype(F32)
            layers_ref[1, h, :, side * 64 : side * 64 + 64] = jnp.where(live, values, 0.0).astype(
                BF16
            )
    outs = adjoint_ref.shape[1] // 2
    for s in range(work):
        row = adjoint_ref[s].astype(F32)
        adjoints[region, s] = jnp.concatenate([row[:outs], row[outs:]], axis=1).astype(BF16)
    greet(region, block, regions, blocks)

    before = lax.rem(block + blocks - 1, blocks)
    after = lax.rem(block + 1, blocks)
    sends = []
    for k in range(1, regions):
        copy = remote(
            adjoints.at[region],
            adjoints.at[region],
            adj_send.at[k],
            adj_recv.at[k],
            (lax.rem(region + k, regions), block),
        )
        copy.start()
        sends.append(copy)
    for k in range(1, blocks):
        copy = remote(
            tags_ref.at[block],
            tags_ref.at[block],
            tag_send.at[k],
            tag_recv.at[k],
            (region, lax.rem(block + k, blocks)),
        )
        copy.start()
        sends.append(copy)
    for i, (slot, target) in enumerate(((2, before), (0, after))):
        copy = remote(
            layers_ref.at[1], layers_ref.at[slot], lay_send.at[i], lay_recv.at[i], (region, target)
        )
        copy.start()
        sends.append(copy)
    for k in range(1, regions):
        source = lax.rem(region + regions - k, regions)
        remote(
            adjoints.at[source],
            adjoints.at[source],
            adj_send.at[k],
            adj_recv.at[k],
            (source, block),
        ).wait_recv()
    for k in range(1, blocks):
        source = lax.rem(block + blocks - k, blocks)
        remote(
            tags_ref.at[source],
            tags_ref.at[source],
            tag_send.at[k],
            tag_recv.at[k],
            (region, source),
        ).wait_recv()
        code = tags_ref[source, pl.ds(block, 1), :]

        def add(j, total, code=code):
            chosen = jnp.where(code == j, 1.0, 0.0)
            return total + chosen * adjoints[lax.div(j, work), lax.rem(j, work)].astype(F32)

        total = lax.fori_loop(
            0, regions * work, add, jnp.zeros(cotangent_ref.shape[1:], F32)
        )
        outgoing[source] = total.astype(BF16)
        copy = remote(
            outgoing.at[source],
            cotangent_ref.at[block],
            cot_send.at[blocks - k],
            cot_recv.at[blocks - k],
            (region, source),
        )
        copy.start()
        sends.append(copy)
    code = tags_ref[block, pl.ds(block, 1), :]

    def add_own(j, total):
        chosen = jnp.where(code == j, 1.0, 0.0)
        return total + chosen * adjoints[lax.div(j, work), lax.rem(j, work)].astype(F32)

    cotangent_ref[block] = lax.fori_loop(
        0, regions * work, add_own, jnp.zeros(cotangent_ref.shape[1:], F32)
    ).astype(BF16)
    for i, (slot, target) in enumerate(((2, after), (0, before))):
        remote(
            layers_ref.at[1], layers_ref.at[slot], lay_send.at[i], lay_recv.at[i], (region, target)
        ).wait_recv()
    for k in range(1, blocks):
        source = lax.rem(block + blocks - k, blocks)
        remote(
            outgoing.at[source],
            cotangent_ref.at[source],
            cot_send.at[k],
            cot_recv.at[k],
            (region, source),
        ).wait_recv()
    for copy in sends:
        copy.wait_send()


def column(ea, eb, ec):
    t = 9 * (ea + 1) + 3 * (eb + 1) + (ec + 1)
    return t if t < 13 else t - 1


def compute_kernel(
    blocks,
    counts_ref,
    rebalance_ref,
    neighbors_ref,
    features_ref,
    layers_ref,
    cotangent_ref,
    weight_ref,
    bias_ref,
    pooled_ref,
    grad_ref,
    bias_grad_ref,
    cubes,
    slabs,
    stacked,
    total,
):
    home, channels = features_ref.shape[0], features_ref.shape[1]
    work = home // 2
    first = (lax.axis_index("region") * blocks + lax.axis_index("block")) * home
    voxel = lax.broadcasted_iota(jnp.int32, (1, 512), 1)
    hashed = (voxel * 167) & 511
    for h in range(home):
        cubes[h] = jnp.where(hashed < counts_ref[h], features_ref[h].astype(F32), 0.0)
        for d in range(3):
            slabs[d * home + h] = layers_ref[d, h].astype(F32)
    cubes[home] = jnp.zeros(cubes.shape[1:], F32)
    slabs[3 * home] = jnp.zeros(slabs.shape[1:], F32)
    total[...] = jnp.zeros_like(total)
    bias_grad_ref[...] = jnp.zeros_like(bias_grad_ref)
    pooled_ref[...] = jnp.zeros_like(pooled_ref)

    v = lax.broadcasted_iota(jnp.int32, (512, 64), 0)
    cell = ((v >> 7) * 4 + ((v >> 4) & 3)) * 4 + ((v & 7) >> 1)
    table = jnp.where(
        cell == lax.broadcasted_iota(jnp.int32, (512, 64), 1), 0.125, 0.0
    ).astype(BF16)
    lane = lax.broadcasted_iota(jnp.int32, (1, 640), 1)
    b_at, c_at = (lane >> 3) & 7, lane & 7
    half = lax.broadcasted_iota(jnp.int32, (1, 128), 1) < 64

    def shifted(x, offset):
        return pltpu.roll(x, (-offset) % 640, 1)

    def one_block(g, carry):
        def slab(ea, fb, fc):
            target = neighbors_ref[g, column(ea, fb, fc)]
            return slabs[jnp.where(target >= 0, target - (first - home), 3 * home)]

        def extended(fb, fc):
            if (fb, fc) == (0, 0):
                middle = cubes[g]
            else:
                target = neighbors_ref[g, column(0, fb, fc)]
                middle = cubes[jnp.where(target >= 0, target - first, home)]
            ends = jnp.where(half, slab(1, fb, fc), slab(-1, fb, fc))
            return jnp.concatenate([middle, ends], axis=1)

        for ec in (-1, 0, 1):
            along = {}
            for fb in (-1, 0, 1):
                if ec == 0:
                    along[fb] = extended(fb, 0)
                else:
                    out = (c_at + ec) != ((c_at + ec) & 7)
                    along[fb] = jnp.where(
                        out,
                        shifted(extended(fb, ec), -7 * ec),
                        shifted(extended(fb, 0), ec),
                    )
            for eb in (-1, 0, 1):
                if eb == 0:
                    plane = along[0]
                else:
                    out = (b_at + eb) != ((b_at + eb) & 7)
                    plane = jnp.where(
                        out, shifted(along[eb], -56 * eb), shifted(along[0], 8 * eb)
                    )
                for ea in (-1, 0, 1):
                    tap = 9 * (ea + 1) + 3 * (eb + 1) + (ec + 1)
                    moved = plane if ea == 0 else shifted(plane, 64 * ea)
                    stacked[tap * channels : (tap + 1) * channels, :] = moved[:, :512].astype(BF16)

        preact = (
            lax.dot_general(
                weight_ref[...],
                stacked[...],
                (((0,), (0,)), ((), ())),
                preferred_element_type=F32,
            )
            + bias_ref[...]
        )
        live = hashed < counts_ref[g]
        gate = jax.nn.sigmoid(preact)
        active = jnp.where(live, preact * gate, 0.0)
        high = active.astype(BF16)
        low = (active - high.astype(F32)).astype(BF16)
        pooled = jnp.dot(high, table, preferred_element_type=F32) + jnp.dot(
            low, table, preferred_element_type=F32
        )
        line = rebalance_ref[g]
        device = jnp.where(line >= 0, lax.rem(lax.div(line, work), blocks), blocks)
        middle = pooled.shape[0] // 2
        pooled_ref[device] = jnp.concatenate([pooled[:middle], pooled[middle:]], axis=1).astype(
            BF16
        )
        row = cotangent_ref[jnp.minimum(device, blocks - 1)].astype(F32)
        width = row.shape[1] // 2
        row = jnp.concatenate([row[:, :width], row[:, width:]], axis=0).astype(BF16)
        spread = lax.dot_general(
            row,
            table,
            (((1,), (1,)), ((), ())),
            preferred_element_type=F32,
        )
        grad = jnp.where(live, spread * gate * (1.0 + preact * (1.0 - gate)), 0.0)
        grad_high = grad.astype(BF16)
        grad_low = (grad - grad_high.astype(F32)).astype(BF16)
        total[...] += lax.dot_general(
            stacked[...], grad_high, (((1,), (1,)), ((), ())), preferred_element_type=F32
        )
        ones = jnp.ones((8, 512), BF16)
        for part in (grad_high, grad_low):
            bias_grad_ref[...] += lax.dot_general(
                ones, part, (((1,), (1,)), ((), ())), preferred_element_type=F32
            )
        return carry

    lax.fori_loop(0, home, one_block, 0)
    used = total.shape[0]
    grad_ref[:used, :] = total[...]
    if grad_ref.shape[0] > used:
        grad_ref[used:, :] = jnp.zeros((grad_ref.shape[0] - used, grad_ref.shape[1]), F32)


def reduce_kernel(
    regions,
    blocks,
    shard,
    pooled_in,
    tags_ref,
    grad_ref,
    bias_ref,
    pooled_ref,
    weight_out,
    bias_out,
    pooled_got,
    pooled_sel,
    pooled_end,
    pair_got,
    pair_sum,
    grad_got,
    grad_part,
    grad_slice,
    grad_full,
    grad_all,
    bias_got,
    bias_part,
    p_send,
    p_recv,
    q_send,
    q_recv,
    e_send,
    e_recv,
    f_send,
    f_recv,
    g_send,
    g_recv,
    h_send,
    h_recv,
    d_send,
    d_recv,
    a_send,
    a_recv,
    b_send,
    b_recv,
    c_send,
    c_recv,
):
    region, block = lax.axis_index("region"), lax.axis_index("block")
    work = pooled_ref.shape[0]
    greet(region, block, regions, blocks)
    sends = []

    def start(*args):
        copy = remote(*args)
        copy.start()
        sends.append(copy)

    def across(k):
        return (region, lax.rem(block + k, blocks))

    def along(k):
        return (lax.rem(region + k, regions), block)

    core, chip, chips = lax.rem(block, 2), lax.div(block, 2), blocks // 2
    sibling = (region, block + 1 - 2 * core)

    def part(side, j):
        index = side * chips + lax.rem(chip + j, chips)
        return pl.ds(pl.multiple_of(index * shard, 16), shard)

    def other_chip(j):
        return (region, 2 * lax.rem(chip + j, chips) + core)

    for k in range(1, blocks):
        peer = lax.rem(block + k, blocks)
        start(pooled_in.at[peer], pooled_got.at[k], p_send.at[k], p_recv.at[k], across(k))
        start(bias_ref, bias_got.at[k], b_send.at[k], b_recv.at[k], across(k))
    for j in (*range(1, chips), 0):
        start(
            grad_ref.at[part(1 - core, j)], pair_got.at[j], e_send.at[j], e_recv.at[j], sibling
        )
    pooled_got[0] = pooled_in[block]
    for j in (*range(1, chips), 0):
        remote(
            grad_ref.at[part(1 - core, j)], pair_got.at[j], e_send.at[j], e_recv.at[j], sibling
        ).wait_recv()
        grad_sum = grad_ref[part(core, j), :] + pair_got[j]
        if j > 0:
            pair_sum[j] = grad_sum.astype(BF16)
            start(pair_sum.at[j], grad_got.at[j], g_send.at[j], g_recv.at[j], other_chip(j))
    for k in range(1, blocks):
        remote(
            pooled_in.at[0], pooled_got.at[k], p_send.at[k], p_recv.at[k], across(k)
        ).wait_recv()

    def select(j, carry):
        def add(k, total):
            code = tags_ref[lax.rem(block + blocks - k, blocks), pl.ds(block, 1), :]
            return total + jnp.where(code == j, 1.0, 0.0) * pooled_got[k].astype(F32)

        total = lax.fori_loop(0, blocks, add, jnp.zeros(pooled_got.shape[1:], F32))
        pooled_sel[lax.div(j, work), lax.rem(j, work)] = total.astype(BF16)
        return carry

    lax.fori_loop(0, regions * work, select, 0)
    for k in range(1, regions):
        peer = lax.rem(region + k, regions)
        start(pooled_sel.at[peer], pooled_end.at[k], q_send.at[k], q_recv.at[k], along(k))
    bias_sum = bias_ref[...]
    for k in range(1, blocks):
        remote(bias_ref, bias_got.at[k], b_send.at[k], b_recv.at[k], across(k)).wait_recv()
        bias_sum = bias_sum + bias_got[k]
    bias_part[region] = bias_sum
    for k in range(1, regions):
        start(
            bias_part.at[region], bias_part.at[region], c_send.at[k], c_recv.at[k], along(k)
        )

    for j in range(1, chips):
        remote(
            pair_sum.at[j], grad_got.at[j], g_send.at[j], g_recv.at[j], other_chip(j)
        ).wait_recv()
        grad_sum = grad_sum + grad_got[j].astype(F32)
    grad_part[...] = grad_sum.reshape(grad_part.shape)
    for k in range(1, regions):
        peer = lax.rem(region + k, regions)
        start(grad_part.at[peer], grad_slice.at[k], h_send.at[k], h_recv.at[k], along(k))
    for k in range(1, regions):
        remote(
            grad_part.at[0], grad_slice.at[k], h_send.at[k], h_recv.at[k], along(k)
        ).wait_recv()
    grad_sum = grad_part[region]
    for k in range(1, regions):
        grad_sum = grad_sum + grad_slice[k]
    grad_full[region] = grad_sum
    for k in range(1, regions):
        start(
            grad_full.at[region], grad_full.at[region], d_send.at[k], d_recv.at[k], along(k)
        )
    for k in range(1, regions):
        source = lax.rem(region + regions - k, regions)
        remote(
            grad_full.at[source], grad_full.at[source], d_send.at[k], d_recv.at[k], along(k)
        ).wait_recv()
    grad_sum = grad_full[...].reshape(shard, -1)
    own = grad_all.at[core, chip]
    own[...] = grad_sum.astype(BF16)
    for j in range(1, chips):
        start(own, own, a_send.at[j], a_recv.at[j], other_chip(j))
    start(own, own, f_send.at[0], f_recv.at[0], sibling)
    for j in range(1, chips):
        slot = grad_all.at[core, lax.rem(chip + chips - j, chips)]
        remote(slot, slot, a_send.at[j], a_recv.at[j], other_chip(j)).wait_recv()
        start(slot, slot, f_send.at[j], f_recv.at[j], sibling)

    for k in range(1, regions):
        source = lax.rem(region + regions - k, regions)
        remote(
            bias_part.at[source], bias_part.at[source], c_send.at[k], c_recv.at[k], along(k)
        ).wait_recv()
        remote(
            pooled_sel.at[0], pooled_end.at[k], q_send.at[k], q_recv.at[k], along(k)
        ).wait_recv()
    bias_sum = bias_part[0]
    for r in range(1, regions):
        bias_sum = bias_sum + bias_part[r]
    bias_out[...] = bias_sum
    for s in range(work):
        rows = pooled_sel[region, s].astype(F32)
        for k in range(1, regions):
            rows = rows + pooled_end[k, s].astype(F32)
        width = rows.shape[1] // 2
        pooled_ref[s] = jnp.concatenate([rows[:, :width], rows[:, width:]], axis=0).astype(BF16)

    for j in range(chips):
        slot = grad_all.at[1 - core, lax.rem(chip + chips - j, chips)]
        remote(slot, slot, f_send.at[j], f_recv.at[j], sibling).wait_recv()
    rows_total = weight_out.shape[0]
    for w in range(blocks):
        low, high = w * shard, min((w + 1) * shard, rows_total)
        if low < high:
            weight_out[low:high, :] = grad_all[w // chips, w % chips, : high - low, :].astype(F32)
    for copy in sends:
        copy.wait_send()


def per_device(
    features,
    counts,
    rebalance,
    neighbors,
    coarse_owner,
    conv_weight,
    convolution_bias_vector,
    merged_adjoint,
):
    home, channels = features.shape[0], features.shape[1]
    taps, _, outs = conv_weight.shape
    work = home // 2
    regions, blocks = lax.axis_size("region"), lax.axis_size("block")
    cells = merged_adjoint.shape[1] // outs
    rows = taps * channels
    dense = (outs // 2, 2 * cells)
    chips = blocks // 2
    unit = math.lcm(16, 8 * regions)
    shard = -(-rows // (blocks * unit)) * unit
    vmem = pl.BlockSpec(memory_space=pltpu.VMEM)
    smem = pl.BlockSpec(memory_space=pltpu.SMEM)
    dma = pltpu.SemaphoreType.DMA
    shape = jax.ShapeDtypeStruct

    layers, cotangent, tags = pl.pallas_call(
        functools.partial(exchange_kernel, regions, blocks),
        out_shape=(
            shape((3, home, channels, 128), BF16),
            shape((blocks,) + dense, BF16),
            shape((blocks, blocks, 128), jnp.int32),
        ),
        in_specs=[smem, smem, smem, vmem, vmem],
        out_specs=(vmem, vmem, vmem),
        scratch_shapes=[
            pltpu.VMEM((regions, work) + dense, BF16),
            pltpu.VMEM((blocks,) + dense, BF16),
            dma((regions,)),
            dma((regions,)),
            dma((blocks,)),
            dma((blocks,)),
            dma((2,)),
            dma((2,)),
            dma((blocks,)),
            dma((blocks,)),
        ],
        compiler_params=pltpu.CompilerParams(
            collective_id=0, has_side_effects=True, vmem_limit_bytes=VMEM_LIMIT
        ),
        name="exchange",
    )(counts, rebalance, coarse_owner, features, merged_adjoint.reshape(work, outs, cells))

    pooled_send, grad_send, bias_send = pl.pallas_call(
        functools.partial(compute_kernel, blocks),
        out_shape=(
            shape((blocks + 1,) + dense, BF16),
            shape((blocks * shard, outs), F32),
            shape((8, outs), F32),
        ),
        in_specs=[smem, smem, smem, vmem, vmem, vmem, vmem, vmem],
        out_specs=(vmem, vmem, vmem),
        scratch_shapes=[
            pltpu.VMEM((home + 1, channels, 512), F32),
            pltpu.VMEM((3 * home + 1, channels, 128), F32),
            pltpu.VMEM((rows, 512), BF16),
            pltpu.VMEM((rows, outs), F32),
        ],
        compiler_params=pltpu.CompilerParams(vmem_limit_bytes=VMEM_LIMIT),
        name="convolve",
    )(
        counts,
        rebalance,
        neighbors,
        features,
        layers,
        cotangent,
        conv_weight.reshape(rows, outs),
        convolution_bias_vector.reshape(outs, 1),
    )

    pooled, weight_total, bias_total = pl.pallas_call(
        functools.partial(reduce_kernel, regions, blocks, shard),
        out_shape=(
            shape((work, outs, cells), BF16),
            shape((rows, outs), F32),
            shape((8, outs), F32),
        ),
        in_specs=[vmem] * 4,
        out_specs=(vmem, vmem, vmem),
        scratch_shapes=[
            pltpu.VMEM((blocks,) + dense, BF16),
            pltpu.VMEM((regions, work) + dense, BF16),
            pltpu.VMEM((regions, work) + dense, BF16),
            pltpu.VMEM((chips, shard, outs), F32),
            pltpu.VMEM((chips, shard, outs), BF16),
            pltpu.VMEM((chips, shard, outs), BF16),
            pltpu.VMEM((regions, shard // regions, outs), F32),
            pltpu.VMEM((regions, shard // regions, outs), F32),
            pltpu.VMEM((regions, shard // regions, outs), F32),
            pltpu.VMEM((2, chips, shard, outs), BF16),
            pltpu.VMEM((blocks, 8, outs), F32),
            pltpu.VMEM((regions, 8, outs), F32),
            dma((blocks,)),
            dma((blocks,)),
            dma((regions,)),
            dma((regions,)),
            dma((chips,)),
            dma((chips,)),
            dma((chips,)),
            dma((chips,)),
            dma((chips,)),
            dma((chips,)),
            dma((regions,)),
            dma((regions,)),
            dma((regions,)),
            dma((regions,)),
            dma((chips,)),
            dma((chips,)),
            dma((blocks,)),
            dma((blocks,)),
            dma((regions,)),
            dma((regions,)),
        ],
        compiler_params=pltpu.CompilerParams(
            collective_id=1, has_side_effects=True, vmem_limit_bytes=VMEM_LIMIT
        ),
        name="reduce",
    )(pooled_send, tags, grad_send, bias_send)
    return (
        pooled.reshape(work, outs * cells),
        weight_total.reshape(taps, channels, outs),
        bias_total[0],
    )


def solution(mesh):
    in_specs = (
        P(("region", "block"), None, None),
        P(("region", "block")),
        P(("region", "block")),
        P(("region", "block"), None),
        P(("region", "block")),
        P(),
        P(),
        P(("region", "block"), None),
    )
    out_specs = (P(("region", "block"), None), P(), P())
    return jax.shard_map(
        per_device, mesh=mesh, in_specs=in_specs, out_specs=out_specs, check_vma=False
    )
```

```python
import functools
import math

import jax
import jax.numpy as jnp
from jax import lax
from jax.experimental import pallas as pl
from jax.experimental.pallas import tpu as pltpu
from jax.sharding import PartitionSpec as P

MESH = pl.DeviceIdType.MESH
VMEM_LIMIT = 48 * 1024 * 1024
F32 = jnp.float32
BF16 = jnp.bfloat16


def greet(region, block, regions, blocks):
    barrier = pltpu.get_barrier_semaphore()
    for k in range(1, blocks):
        pl.semaphore_signal(
            barrier, inc=1, device_id=(region, lax.rem(block + k, blocks)), device_id_type=MESH
        )
    for k in range(1, regions):
        pl.semaphore_signal(
            barrier, inc=1, device_id=(lax.rem(region + k, regions), block), device_id_type=MESH
        )
    pl.semaphore_wait(barrier, blocks + regions - 2)


def remote(src, dst, send_sem, recv_sem, device):
    return pltpu.make_async_remote_copy(
        src_ref=src,
        dst_ref=dst,
        send_sem=send_sem,
        recv_sem=recv_sem,
        device_id=device,
        device_id_type=MESH,
    )


def exchange_kernel(
    regions,
    blocks,
    counts_ref,
    rebalance_ref,
    owner_ref,
    features_ref,
    adjoint_ref,
    layers_ref,
    cotangent_ref,
    mine_ref,
    tags_ref,
    codes_ref,
    adjoints,
    outgoing,
    code_sem,
    adj_send,
    adj_recv,
    tag_send,
    tag_recv,
    lay_send,
    lay_recv,
    cot_send,
    cot_recv,
):
    region, block = lax.axis_index("region"), lax.axis_index("block")
    home = features_ref.shape[0]
    work = adjoint_ref.shape[0]
    rows = lax.broadcasted_iota(jnp.int32, (blocks, 128), 0)
    codes = jnp.full((blocks, 128), -1, jnp.int32)
    for h in range(home):
        line = rebalance_ref[h]
        device = jnp.where(line >= 0, lax.rem(lax.div(line, work), blocks), -1)
        code = owner_ref[h] * work + lax.rem(line, work)
        codes = jnp.where(rows == device, code, codes)
    tags_ref[block] = codes
    lanes = lax.broadcasted_iota(jnp.int32, (1, 64), 1)
    for h in range(home):
        for side, start in enumerate((0, 448)):
            live = (((lanes + start) * 167) & 511) < counts_ref[h]
            values = features_ref[h, :, start : start + 64].astype(F32)
            layers_ref[1, h, :, side * 64 : side * 64 + 64] = jnp.where(live, values, 0.0).astype(
                BF16
            )
    outs = adjoint_ref.shape[1] // 2
    for s in range(work):
        row = adjoint_ref[s].astype(F32)
        adjoints[region * work + s] = jnp.concatenate([row[:outs], row[outs:]], axis=1).astype(BF16)
    greet(region, block, regions, blocks)

    before = lax.rem(block + blocks - 1, blocks)
    after = lax.rem(block + 1, blocks)
    sends = []
    for k in range(1, regions):
        copy = remote(
            adjoints.at[pl.ds(region * work, work)],
            adjoints.at[pl.ds(region * work, work)],
            adj_send.at[k],
            adj_recv.at[k],
            (lax.rem(region + k, regions), block),
        )
        copy.start()
        sends.append(copy)
    for k in range(1, blocks):
        copy = remote(
            tags_ref.at[block],
            tags_ref.at[block],
            tag_send.at[k],
            tag_recv.at[k],
            (region, lax.rem(block + k, blocks)),
        )
        copy.start()
        sends.append(copy)
    for i, (slot, target) in enumerate(((2, before), (0, after))):
        copy = remote(
            layers_ref.at[1], layers_ref.at[slot], lay_send.at[i], lay_recv.at[i], (region, target)
        )
        copy.start()
        sends.append(copy)
    for k in range(1, blocks):
        source = lax.rem(block + blocks - k, blocks)
        remote(
            tags_ref.at[source],
            tags_ref.at[source],
            tag_send.at[k],
            tag_recv.at[k],
            (region, source),
        ).wait_recv()
        mine_ref[pl.ds(source, 1), :] = tags_ref[source, pl.ds(block, 1), :]
    mine_ref[pl.ds(block, 1), :] = tags_ref[block, pl.ds(block, 1), :]
    codes_copy = pltpu.make_async_copy(mine_ref, codes_ref, code_sem)
    codes_copy.start()
    codes_copy.wait()
    for k in range(1, regions):
        source = lax.rem(region + regions - k, regions)
        remote(
            adjoints.at[pl.ds(source * work, work)],
            adjoints.at[pl.ds(source * work, work)],
            adj_send.at[k],
            adj_recv.at[k],
            (source, block),
        ).wait_recv()
    for k in range(1, blocks):
        source = lax.rem(block + blocks - k, blocks)
        outgoing[source] = adjoints[jnp.maximum(codes_ref[source, 0], 0)]
        copy = remote(
            outgoing.at[source],
            cotangent_ref.at[block],
            cot_send.at[blocks - k],
            cot_recv.at[blocks - k],
            (region, source),
        )
        copy.start()
        sends.append(copy)
    cotangent_ref[block] = adjoints[jnp.maximum(codes_ref[block, 0], 0)]
    for i, (slot, target) in enumerate(((2, after), (0, before))):
        remote(
            layers_ref.at[1], layers_ref.at[slot], lay_send.at[i], lay_recv.at[i], (region, target)
        ).wait_recv()
    for k in range(1, blocks):
        source = lax.rem(block + blocks - k, blocks)
        remote(
            outgoing.at[source],
            cotangent_ref.at[source],
            cot_send.at[k],
            cot_recv.at[k],
            (region, source),
        ).wait_recv()
    for copy in sends:
        copy.wait_send()


def column(ea, eb, ec):
    t = 9 * (ea + 1) + 3 * (eb + 1) + (ec + 1)
    return t if t < 13 else t - 1


def compute_kernel(
    blocks,
    counts_ref,
    rebalance_ref,
    neighbors_ref,
    features_ref,
    layers_ref,
    cotangent_ref,
    weight_ref,
    bias_ref,
    pooled_ref,
    grad_ref,
    bias_grad_ref,
    cubes,
    slabs,
    stacked,
    total,
):
    home, channels = features_ref.shape[0], features_ref.shape[1]
    work = home // 2
    first = (lax.axis_index("region") * blocks + lax.axis_index("block")) * home
    voxel = lax.broadcasted_iota(jnp.int32, (1, 512), 1)
    hashed = (voxel * 167) & 511
    for h in range(home):
        cubes[h] = jnp.where(hashed < counts_ref[h], features_ref[h].astype(F32), 0.0)
        for d in range(3):
            slabs[d * home + h] = layers_ref[d, h].astype(F32)
    cubes[home] = jnp.zeros(cubes.shape[1:], F32)
    slabs[3 * home] = jnp.zeros(slabs.shape[1:], F32)
    total[...] = jnp.zeros_like(total)
    bias_grad_ref[...] = jnp.zeros_like(bias_grad_ref)
    pooled_ref[...] = jnp.zeros_like(pooled_ref)

    v = lax.broadcasted_iota(jnp.int32, (512, 64), 0)
    cell = ((v >> 7) * 4 + ((v >> 4) & 3)) * 4 + ((v & 7) >> 1)
    table = jnp.where(
        cell == lax.broadcasted_iota(jnp.int32, (512, 64), 1), 0.125, 0.0
    ).astype(BF16)
    lane = lax.broadcasted_iota(jnp.int32, (1, 640), 1)
    b_at, c_at = (lane >> 3) & 7, lane & 7
    half = lax.broadcasted_iota(jnp.int32, (1, 128), 1) < 64

    def shifted(x, offset):
        return pltpu.roll(x, (-offset) % 640, 1)

    def one_block(g, carry):
        def slab(ea, fb, fc):
            target = neighbors_ref[g, column(ea, fb, fc)]
            return slabs[jnp.where(target >= 0, target - (first - home), 3 * home)]

        def extended(fb, fc):
            if (fb, fc) == (0, 0):
                middle = cubes[g]
            else:
                target = neighbors_ref[g, column(0, fb, fc)]
                middle = cubes[jnp.where(target >= 0, target - first, home)]
            ends = jnp.where(half, slab(1, fb, fc), slab(-1, fb, fc))
            return jnp.concatenate([middle, ends], axis=1)

        for ec in (-1, 0, 1):
            along = {}
            for fb in (-1, 0, 1):
                if ec == 0:
                    along[fb] = extended(fb, 0)
                else:
                    out = (c_at + ec) != ((c_at + ec) & 7)
                    along[fb] = jnp.where(
                        out,
                        shifted(extended(fb, ec), -7 * ec),
                        shifted(extended(fb, 0), ec),
                    )
            for eb in (-1, 0, 1):
                if eb == 0:
                    plane = along[0]
                else:
                    out = (b_at + eb) != ((b_at + eb) & 7)
                    plane = jnp.where(
                        out, shifted(along[eb], -56 * eb), shifted(along[0], 8 * eb)
                    )
                for ea in (-1, 0, 1):
                    tap = 9 * (ea + 1) + 3 * (eb + 1) + (ec + 1)
                    moved = plane if ea == 0 else shifted(plane, 64 * ea)
                    stacked[tap * channels : (tap + 1) * channels, :] = moved[:, :512].astype(BF16)

        preact = (
            lax.dot_general(
                weight_ref[...],
                stacked[...],
                (((0,), (0,)), ((), ())),
                preferred_element_type=F32,
            )
            + bias_ref[...]
        )
        live = hashed < counts_ref[g]
        gate = jax.nn.sigmoid(preact)
        active = jnp.where(live, preact * gate, 0.0)
        high = active.astype(BF16)
        low = (active - high.astype(F32)).astype(BF16)
        pooled = jnp.dot(high, table, preferred_element_type=F32) + jnp.dot(
            low, table, preferred_element_type=F32
        )
        line = rebalance_ref[g]
        device = jnp.where(line >= 0, lax.rem(lax.div(line, work), blocks), blocks)
        middle = pooled.shape[0] // 2
        pooled_ref[device] = jnp.concatenate([pooled[:middle], pooled[middle:]], axis=1).astype(
            BF16
        )
        row = cotangent_ref[jnp.minimum(device, blocks - 1)].astype(F32)
        width = row.shape[1] // 2
        row = jnp.concatenate([row[:, :width], row[:, width:]], axis=0).astype(BF16)
        spread = lax.dot_general(
            row,
            table,
            (((1,), (1,)), ((), ())),
            preferred_element_type=F32,
        )
        grad = jnp.where(live, spread * gate * (1.0 + preact * (1.0 - gate)), 0.0)
        grad_high = grad.astype(BF16)
        grad_low = (grad - grad_high.astype(F32)).astype(BF16)
        total[...] += lax.dot_general(
            stacked[...], grad_high, (((1,), (1,)), ((), ())), preferred_element_type=F32
        )
        ones = jnp.ones((8, 512), BF16)
        for part in (grad_high, grad_low):
            bias_grad_ref[...] += lax.dot_general(
                ones, part, (((1,), (1,)), ((), ())), preferred_element_type=F32
            )
        return carry

    lax.fori_loop(0, home, one_block, 0)
    used = total.shape[0]
    grad_ref[:used, :] = total[...]
    if grad_ref.shape[0] > used:
        grad_ref[used:, :] = jnp.zeros((grad_ref.shape[0] - used, grad_ref.shape[1]), F32)


def reduce_kernel(
    regions,
    blocks,
    shard,
    pooled_in,
    codes_ref,
    grad_ref,
    bias_ref,
    pooled_ref,
    weight_out,
    bias_out,
    pooled_got,
    pooled_sel,
    pooled_end,
    pair_got,
    pair_sum,
    grad_got,
    grad_part,
    grad_slice,
    grad_full,
    grad_all,
    bias_got,
    bias_part,
    p_send,
    p_recv,
    q_send,
    q_recv,
    e_send,
    e_recv,
    f_send,
    f_recv,
    g_send,
    g_recv,
    h_send,
    h_recv,
    d_send,
    d_recv,
    a_send,
    a_recv,
    b_send,
    b_recv,
    c_send,
    c_recv,
):
    region, block = lax.axis_index("region"), lax.axis_index("block")
    work = pooled_ref.shape[0]
    greet(region, block, regions, blocks)
    sends = []

    def start(*args):
        copy = remote(*args)
        copy.start()
        sends.append(copy)

    def across(k):
        return (region, lax.rem(block + k, blocks))

    def along(k):
        return (lax.rem(region + k, regions), block)

    core, chip, chips = lax.rem(block, 2), lax.div(block, 2), blocks // 2
    sibling = (region, block + 1 - 2 * core)

    def part(side, j):
        index = side * chips + lax.rem(chip + j, chips)
        return pl.ds(pl.multiple_of(index * shard, 16), shard)

    def other_chip(j):
        return (region, 2 * lax.rem(chip + j, chips) + core)

    for k in range(1, blocks):
        peer = lax.rem(block + k, blocks)
        start(pooled_in.at[peer], pooled_got.at[k], p_send.at[k], p_recv.at[k], across(k))
        start(bias_ref, bias_got.at[k], b_send.at[k], b_recv.at[k], across(k))
    for j in (*range(1, chips), 0):
        start(
            grad_ref.at[part(1 - core, j)], pair_got.at[j], e_send.at[j], e_recv.at[j], sibling
        )
    pooled_got[0] = pooled_in[block]
    for j in (*range(1, chips), 0):
        remote(
            grad_ref.at[part(1 - core, j)], pair_got.at[j], e_send.at[j], e_recv.at[j], sibling
        ).wait_recv()
        grad_sum = grad_ref[part(core, j), :] + pair_got[j]
        if j > 0:
            pair_sum[j] = grad_sum.astype(BF16)
            start(pair_sum.at[j], grad_got.at[j], g_send.at[j], g_recv.at[j], other_chip(j))
    for k in range(1, blocks):
        remote(
            pooled_in.at[0], pooled_got.at[k], p_send.at[k], p_recv.at[k], across(k)
        ).wait_recv()

    def select(j, carry):
        slot, found = 0, 0.0
        for k in range(blocks):
            hit = codes_ref[lax.rem(block + blocks - k, blocks), 0] == j
            slot = jnp.where(hit, k, slot)
            found = jnp.where(hit, 1.0, found)
        total = pooled_got[slot].astype(F32) * found
        pooled_sel[lax.div(j, work), lax.rem(j, work)] = total.astype(BF16)
        return carry

    lax.fori_loop(0, regions * work, select, 0)
    for k in range(1, regions):
        peer = lax.rem(region + k, regions)
        start(pooled_sel.at[peer], pooled_end.at[k], q_send.at[k], q_recv.at[k], along(k))
    bias_sum = bias_ref[...]
    for k in range(1, blocks):
        remote(bias_ref, bias_got.at[k], b_send.at[k], b_recv.at[k], across(k)).wait_recv()
        bias_sum = bias_sum + bias_got[k]
    bias_part[region] = bias_sum
    for k in range(1, regions):
        start(
            bias_part.at[region], bias_part.at[region], c_send.at[k], c_recv.at[k], along(k)
        )

    for j in range(1, chips):
        remote(
            pair_sum.at[j], grad_got.at[j], g_send.at[j], g_recv.at[j], other_chip(j)
        ).wait_recv()
        grad_sum = grad_sum + grad_got[j].astype(F32)
    grad_part[...] = grad_sum.reshape(grad_part.shape)
    for k in range(1, regions):
        peer = lax.rem(region + k, regions)
        start(grad_part.at[peer], grad_slice.at[k], h_send.at[k], h_recv.at[k], along(k))
    for k in range(1, regions):
        remote(
            grad_part.at[0], grad_slice.at[k], h_send.at[k], h_recv.at[k], along(k)
        ).wait_recv()
    grad_sum = grad_part[region]
    for k in range(1, regions):
        grad_sum = grad_sum + grad_slice[k]
    grad_full[region] = grad_sum
    for k in range(1, regions):
        start(
            grad_full.at[region], grad_full.at[region], d_send.at[k], d_recv.at[k], along(k)
        )
    for k in range(1, regions):
        source = lax.rem(region + regions - k, regions)
        remote(
            grad_full.at[source], grad_full.at[source], d_send.at[k], d_recv.at[k], along(k)
        ).wait_recv()
    grad_sum = grad_full[...].reshape(shard, -1)
    own = grad_all.at[core, chip]
    own[...] = grad_sum.astype(BF16)
    for j in range(1, chips):
        start(own, own, a_send.at[j], a_recv.at[j], other_chip(j))
    start(own, own, f_send.at[0], f_recv.at[0], sibling)
    for j in range(1, chips):
        slot = grad_all.at[core, lax.rem(chip + chips - j, chips)]
        remote(slot, slot, a_send.at[j], a_recv.at[j], other_chip(j)).wait_recv()
        start(slot, slot, f_send.at[j], f_recv.at[j], sibling)

    for k in range(1, regions):
        source = lax.rem(region + regions - k, regions)
        remote(
            bias_part.at[source], bias_part.at[source], c_send.at[k], c_recv.at[k], along(k)
        ).wait_recv()
        remote(
            pooled_sel.at[0], pooled_end.at[k], q_send.at[k], q_recv.at[k], along(k)
        ).wait_recv()
    bias_sum = bias_part[0]
    for r in range(1, regions):
        bias_sum = bias_sum + bias_part[r]
    bias_out[...] = bias_sum
    for s in range(work):
        rows = pooled_sel[region, s].astype(F32)
        for k in range(1, regions):
            rows = rows + pooled_end[k, s].astype(F32)
        width = rows.shape[1] // 2
        pooled_ref[s] = jnp.concatenate([rows[:, :width], rows[:, width:]], axis=0).astype(BF16)

    for j in range(chips):
        slot = grad_all.at[1 - core, lax.rem(chip + chips - j, chips)]
        remote(slot, slot, f_send.at[j], f_recv.at[j], sibling).wait_recv()
    rows_total = weight_out.shape[0]
    for w in range(blocks):
        low, high = w * shard, min((w + 1) * shard, rows_total)
        if low < high:
            weight_out[low:high, :] = grad_all[w // chips, w % chips, : high - low, :].astype(F32)
    for copy in sends:
        copy.wait_send()


def per_device(
    features,
    counts,
    rebalance,
    neighbors,
    coarse_owner,
    conv_weight,
    convolution_bias_vector,
    merged_adjoint,
):
    home, channels = features.shape[0], features.shape[1]
    taps, _, outs = conv_weight.shape
    work = home // 2
    regions, blocks = lax.axis_size("region"), lax.axis_size("block")
    cells = merged_adjoint.shape[1] // outs
    rows = taps * channels
    dense = (outs // 2, 2 * cells)
    chips = blocks // 2
    unit = math.lcm(16, 8 * regions)
    shard = -(-rows // (blocks * unit)) * unit
    vmem = pl.BlockSpec(memory_space=pltpu.VMEM)
    smem = pl.BlockSpec(memory_space=pltpu.SMEM)
    dma = pltpu.SemaphoreType.DMA
    shape = jax.ShapeDtypeStruct

    layers, cotangent, codes = pl.pallas_call(
        functools.partial(exchange_kernel, regions, blocks),
        out_shape=(
            shape((3, home, channels, 128), BF16),
            shape((blocks,) + dense, BF16),
            shape((blocks, 128), jnp.int32),
        ),
        in_specs=[smem, smem, smem, vmem, vmem],
        out_specs=(vmem, vmem, vmem),
        scratch_shapes=[
            pltpu.VMEM((blocks, blocks, 128), jnp.int32),
            pltpu.SMEM((blocks, 128), jnp.int32),
            pltpu.VMEM((regions * work,) + dense, BF16),
            pltpu.VMEM((blocks,) + dense, BF16),
            dma,
            dma((regions,)),
            dma((regions,)),
            dma((blocks,)),
            dma((blocks,)),
            dma((2,)),
            dma((2,)),
            dma((blocks,)),
            dma((blocks,)),
        ],
        compiler_params=pltpu.CompilerParams(
            collective_id=0, has_side_effects=True, vmem_limit_bytes=VMEM_LIMIT
        ),
        name="exchange",
    )(counts, rebalance, coarse_owner, features, merged_adjoint.reshape(work, outs, cells))

    pooled_send, grad_send, bias_send = pl.pallas_call(
        functools.partial(compute_kernel, blocks),
        out_shape=(
            shape((blocks + 1,) + dense, BF16),
            shape((blocks * shard, outs), F32),
            shape((8, outs), F32),
        ),
        in_specs=[smem, smem, smem, vmem, vmem, vmem, vmem, vmem],
        out_specs=(vmem, vmem, vmem),
        scratch_shapes=[
            pltpu.VMEM((home + 1, channels, 512), F32),
            pltpu.VMEM((3 * home + 1, channels, 128), F32),
            pltpu.VMEM((rows, 512), BF16),
            pltpu.VMEM((rows, outs), F32),
        ],
        compiler_params=pltpu.CompilerParams(vmem_limit_bytes=VMEM_LIMIT),
        name="convolve",
    )(
        counts,
        rebalance,
        neighbors,
        features,
        layers,
        cotangent,
        conv_weight.reshape(rows, outs),
        convolution_bias_vector.reshape(outs, 1),
    )

    pooled, weight_total, bias_total = pl.pallas_call(
        functools.partial(reduce_kernel, regions, blocks, shard),
        out_shape=(
            shape((work, outs, cells), BF16),
            shape((rows, outs), F32),
            shape((8, outs), F32),
        ),
        in_specs=[vmem, smem, vmem, vmem],
        out_specs=(vmem, vmem, vmem),
        scratch_shapes=[
            pltpu.VMEM((blocks,) + dense, BF16),
            pltpu.VMEM((regions, work) + dense, BF16),
            pltpu.VMEM((regions, work) + dense, BF16),
            pltpu.VMEM((chips, shard, outs), F32),
            pltpu.VMEM((chips, shard, outs), BF16),
            pltpu.VMEM((chips, shard, outs), BF16),
            pltpu.VMEM((regions, shard // regions, outs), F32),
            pltpu.VMEM((regions, shard // regions, outs), F32),
            pltpu.VMEM((regions, shard // regions, outs), F32),
            pltpu.VMEM((2, chips, shard, outs), BF16),
            pltpu.VMEM((blocks, 8, outs), F32),
            pltpu.VMEM((regions, 8, outs), F32),
            dma((blocks,)),
            dma((blocks,)),
            dma((regions,)),
            dma((regions,)),
            dma((chips,)),
            dma((chips,)),
            dma((chips,)),
            dma((chips,)),
            dma((chips,)),
            dma((chips,)),
            dma((regions,)),
            dma((regions,)),
            dma((regions,)),
            dma((regions,)),
            dma((chips,)),
            dma((chips,)),
            dma((blocks,)),
            dma((blocks,)),
            dma((regions,)),
            dma((regions,)),
        ],
        compiler_params=pltpu.CompilerParams(
            collective_id=1, has_side_effects=True, vmem_limit_bytes=VMEM_LIMIT
        ),
        name="reduce",
    )(pooled_send, codes, grad_send, bias_send)
    return (
        pooled.reshape(work, outs * cells),
        weight_total.reshape(taps, channels, outs),
        bias_total[0],
    )


def solution(mesh):
    in_specs = (
        P(("region", "block"), None, None),
        P(("region", "block")),
        P(("region", "block")),
        P(("region", "block"), None),
        P(("region", "block")),
        P(),
        P(),
        P(("region", "block"), None),
    )
    out_specs = (P(("region", "block"), None), P(), P())
    return jax.shard_map(
        per_device, mesh=mesh, in_specs=in_specs, out_specs=out_specs, check_vma=False
    )
```

```python
import functools
import math

import jax
import jax.numpy as jnp
from jax import lax
from jax.experimental import pallas as pl
from jax.experimental.pallas import tpu as pltpu
from jax.sharding import PartitionSpec as P

MESH = pl.DeviceIdType.MESH
VMEM_LIMIT = 48 * 1024 * 1024
F32 = jnp.float32
BF16 = jnp.bfloat16


def greet(region, block, regions, blocks):
    barrier = pltpu.get_barrier_semaphore()
    for k in range(1, blocks):
        pl.semaphore_signal(
            barrier, inc=1, device_id=(region, lax.rem(block + k, blocks)), device_id_type=MESH
        )
    for k in range(1, regions):
        pl.semaphore_signal(
            barrier, inc=1, device_id=(lax.rem(region + k, regions), block), device_id_type=MESH
        )
    pl.semaphore_wait(barrier, blocks + regions - 2)


def remote(src, dst, send_sem, recv_sem, device):
    return pltpu.make_async_remote_copy(
        src_ref=src,
        dst_ref=dst,
        send_sem=send_sem,
        recv_sem=recv_sem,
        device_id=device,
        device_id_type=MESH,
    )


def column(ea, eb, ec):
    t = 9 * (ea + 1) + 3 * (eb + 1) + (ec + 1)
    return t if t < 13 else t - 1


def fused_kernel(
    regions,
    blocks,
    shard,
    counts_ref,
    rebalance_ref,
    owner_ref,
    neighbors_ref,
    features_ref,
    adjoint_ref,
    weight_ref,
    conv_bias_ref,
    pooled_ref,
    weight_out,
    bias_out,
    layers_ref,
    cotangent_ref,
    mine_ref,
    tags_ref,
    codes_ref,
    adjoints,
    outgoing,
    cubes,
    slabs,
    stacked,
    preacts,
    pooled_block,
    pooled_in,
    grad_ref,
    bias_ref,
    pooled_got,
    pooled_sel,
    pooled_end,
    pair_got,
    pair_sum,
    grad_got,
    grad_part,
    grad_slice,
    grad_full,
    grad_all,
    bias_got,
    bias_part,
    code_sem,
    lay_send,
    lay_recv,
    adj_send,
    adj_recv,
    q_send,
    q_recv,
    h_send,
    h_recv,
    d_send,
    d_recv,
    c_send,
    c_recv,
    tag_send,
    tag_recv,
    cot_send,
    cot_recv,
    p_send,
    p_recv,
    b_send,
    b_recv,
    e_send,
    e_recv,
    f_send,
    f_recv,
    g_send,
    g_recv,
    a_send,
    a_recv,
):
    region, block = lax.axis_index("region"), lax.axis_index("block")
    home = features_ref.shape[0]
    work = adjoint_ref.shape[0]
    rows = lax.broadcasted_iota(jnp.int32, (blocks, 128), 0)
    codes = jnp.full((blocks, 128), -1, jnp.int32)
    for h in range(home):
        line = rebalance_ref[h]
        device = jnp.where(line >= 0, lax.rem(lax.div(line, work), blocks), -1)
        code = owner_ref[h] * work + lax.rem(line, work)
        codes = jnp.where(rows == device, code, codes)
    tags_ref[block] = codes
    lanes = lax.broadcasted_iota(jnp.int32, (1, 64), 1)
    for h in range(home):
        for side, start in enumerate((0, 448)):
            live = (((lanes + start) * 167) & 511) < counts_ref[h]
            values = features_ref[h, :, start : start + 64].astype(F32)
            layers_ref[1, h, :, side * 64 : side * 64 + 64] = jnp.where(live, values, 0.0).astype(
                BF16
            )
    outs = adjoint_ref.shape[1] // 2
    for s in range(work):
        row = adjoint_ref[s].astype(F32)
        adjoints[region * work + s] = jnp.concatenate([row[:outs], row[outs:]], axis=1).astype(BF16)
    greet(region, block, regions, blocks)

    before = lax.rem(block + blocks - 1, blocks)
    after = lax.rem(block + 1, blocks)
    sends = []

    def start(*args):
        copy = remote(*args)
        copy.start()
        sends.append(copy)

    def across(k):
        return (region, lax.rem(block + k, blocks))

    def along(k):
        return (lax.rem(region + k, regions), block)

    core, chip, chips = lax.rem(block, 2), lax.div(block, 2), blocks // 2
    sibling = (region, block + 1 - 2 * core)

    def part(side, j):
        index = side * chips + lax.rem(chip + j, chips)
        return pl.ds(pl.multiple_of(index * shard, 16), shard)

    def other_chip(j):
        return (region, 2 * lax.rem(chip + j, chips) + core)

    for k in range(1, regions):
        copy = remote(
            adjoints.at[pl.ds(region * work, work)],
            adjoints.at[pl.ds(region * work, work)],
            adj_send.at[k],
            adj_recv.at[k],
            (lax.rem(region + k, regions), block),
        )
        copy.start()
        sends.append(copy)
    for k in range(1, blocks):
        copy = remote(
            tags_ref.at[block],
            tags_ref.at[block],
            tag_send.at[k],
            tag_recv.at[k],
            (region, lax.rem(block + k, blocks)),
        )
        copy.start()
        sends.append(copy)
    for i, (slot, target) in enumerate(((2, before), (0, after))):
        copy = remote(
            layers_ref.at[1], layers_ref.at[slot], lay_send.at[i], lay_recv.at[i], (region, target)
        )
        copy.start()
        sends.append(copy)
    for k in range(1, blocks):
        source = lax.rem(block + blocks - k, blocks)
        remote(
            tags_ref.at[source],
            tags_ref.at[source],
            tag_send.at[k],
            tag_recv.at[k],
            (region, source),
        ).wait_recv()
        mine_ref[pl.ds(source, 1), :] = tags_ref[source, pl.ds(block, 1), :]
    mine_ref[pl.ds(block, 1), :] = tags_ref[block, pl.ds(block, 1), :]
    codes_copy = pltpu.make_async_copy(mine_ref, codes_ref, code_sem)
    codes_copy.start()
    codes_copy.wait()
    for k in range(1, regions):
        source = lax.rem(region + regions - k, regions)
        remote(
            adjoints.at[pl.ds(source * work, work)],
            adjoints.at[pl.ds(source * work, work)],
            adj_send.at[k],
            adj_recv.at[k],
            (source, block),
        ).wait_recv()
    for k in range(1, blocks):
        source = lax.rem(block + blocks - k, blocks)
        outgoing[source] = adjoints[jnp.clip(codes_ref[source, 0], 0, regions * work - 1)]
        copy = remote(
            outgoing.at[source],
            cotangent_ref.at[block],
            cot_send.at[blocks - k],
            cot_recv.at[blocks - k],
            (region, source),
        )
        copy.start()
        sends.append(copy)
    cotangent_ref[block] = adjoints[jnp.clip(codes_ref[block, 0], 0, regions * work - 1)]
    for i, (slot, target) in enumerate(((2, after), (0, before))):
        remote(
            layers_ref.at[1], layers_ref.at[slot], lay_send.at[i], lay_recv.at[i], (region, target)
        ).wait_recv()
    channels = features_ref.shape[1]
    first = (region * blocks + block) * home
    voxel = lax.broadcasted_iota(jnp.int32, (1, 512), 1)
    hashed = (voxel * 167) & 511
    for h in range(home):
        cubes[h] = jnp.where(hashed < counts_ref[h], features_ref[h].astype(F32), 0.0)
        for d in range(3):
            slabs[d * home + h] = layers_ref[d, h].astype(F32)
    cubes[home] = jnp.zeros(cubes.shape[1:], F32)
    slabs[3 * home] = jnp.zeros(slabs.shape[1:], F32)
    used = weight_ref.shape[0]
    grad_ref[...] = jnp.zeros_like(grad_ref)
    bias_ref[...] = jnp.zeros_like(bias_ref)

    v = lax.broadcasted_iota(jnp.int32, (512, 64), 0)
    cell = ((v >> 7) * 4 + ((v >> 4) & 3)) * 4 + ((v & 7) >> 1)
    table = jnp.where(
        cell == lax.broadcasted_iota(jnp.int32, (512, 64), 1), 0.125, 0.0
    ).astype(BF16)
    lane = lax.broadcasted_iota(jnp.int32, (1, 640), 1)
    b_at, c_at = (lane >> 3) & 7, lane & 7
    half = lax.broadcasted_iota(jnp.int32, (1, 128), 1) < 64

    def shifted(x, offset):
        return pltpu.roll(x, (-offset) % 640, 1)

    def forward(g, carry):
        def slab(ea, fb, fc):
            target = neighbors_ref[g, column(ea, fb, fc)]
            return slabs[jnp.where(target >= 0, jnp.clip(target - (first - home), 0, 3 * home - 1), 3 * home)]

        def extended(fb, fc):
            if (fb, fc) == (0, 0):
                middle = cubes[g]
            else:
                target = neighbors_ref[g, column(0, fb, fc)]
                middle = cubes[jnp.where(target >= 0, jnp.clip(target - first, 0, home - 1), home)]
            ends = jnp.where(half, slab(1, fb, fc), slab(-1, fb, fc))
            return jnp.concatenate([middle, ends], axis=1)

        for ec in (-1, 0, 1):
            along = {}
            for fb in (-1, 0, 1):
                if ec == 0:
                    along[fb] = extended(fb, 0)
                else:
                    out = (c_at + ec) != ((c_at + ec) & 7)
                    along[fb] = jnp.where(
                        out,
                        shifted(extended(fb, ec), -7 * ec),
                        shifted(extended(fb, 0), ec),
                    )
            for eb in (-1, 0, 1):
                if eb == 0:
                    plane = along[0]
                else:
                    out = (b_at + eb) != ((b_at + eb) & 7)
                    plane = jnp.where(
                        out, shifted(along[eb], -56 * eb), shifted(along[0], 8 * eb)
                    )
                for ea in (-1, 0, 1):
                    tap = 9 * (ea + 1) + 3 * (eb + 1) + (ec + 1)
                    moved = plane if ea == 0 else shifted(plane, 64 * ea)
                    stacked[g, tap * channels : (tap + 1) * channels, :] = moved[:, :512].astype(BF16)

        preact = (
            lax.dot_general(
                weight_ref[...],
                stacked[g],
                (((0,), (0,)), ((), ())),
                preferred_element_type=F32,
            )
            + conv_bias_ref[...]
        )
        live = hashed < counts_ref[g]
        gate = jax.nn.sigmoid(preact)
        active = jnp.where(live, preact * gate, 0.0)
        high = active.astype(BF16)
        low = (active - high.astype(F32)).astype(BF16)
        pooled = jnp.dot(high, table, preferred_element_type=F32) + jnp.dot(
            low, table, preferred_element_type=F32
        )
        middle = pooled.shape[0] // 2
        pooled_block[g] = jnp.concatenate([pooled[:middle], pooled[middle:]], axis=1).astype(
            BF16
        )
        preacts[g] = preact
        return carry

    lax.fori_loop(0, home, forward, 0)
    for w in range(blocks):
        slot = 0
        for h in range(home):
            line = rebalance_ref[h]
            hit = (line >= 0) & (lax.rem(lax.div(line, work), blocks) == w)
            slot = jnp.where(hit, h, slot)
        pooled_in[w] = pooled_block[slot]
    for k in range(1, blocks):
        peer = lax.rem(block + k, blocks)
        start(pooled_in.at[peer], pooled_got.at[k], p_send.at[k], p_recv.at[k], across(k))
    pooled_got[0] = pooled_in[block]
    for k in range(1, blocks):
        source = lax.rem(block + blocks - k, blocks)
        remote(
            outgoing.at[source],
            cotangent_ref.at[source],
            cot_send.at[k],
            cot_recv.at[k],
            (region, source),
        ).wait_recv()

    def backward(g, carry):
        preact = preacts[g]
        live = hashed < counts_ref[g]
        gate = jax.nn.sigmoid(preact)
        line = jnp.maximum(rebalance_ref[g], 0)
        device = lax.rem(lax.div(line, work), blocks)
        row = cotangent_ref[device].astype(F32)
        width = row.shape[1] // 2
        row = jnp.concatenate([row[:, :width], row[:, width:]], axis=0).astype(BF16)
        spread = lax.dot_general(
            row,
            table,
            (((1,), (1,)), ((), ())),
            preferred_element_type=F32,
        )
        grad = jnp.where(live, spread * gate * (1.0 + preact * (1.0 - gate)), 0.0)
        grad_high = grad.astype(BF16)
        grad_low = (grad - grad_high.astype(F32)).astype(BF16)
        grad_ref[:used, :] += lax.dot_general(
            stacked[g], grad_high, (((1,), (1,)), ((), ())), preferred_element_type=F32
        )
        ones = jnp.ones((8, 512), BF16)
        for part in (grad_high, grad_low):
            bias_ref[...] += lax.dot_general(
                ones, part, (((1,), (1,)), ((), ())), preferred_element_type=F32
            )
        return carry

    lax.fori_loop(0, home, backward, 0)
    for k in range(1, blocks):
        start(bias_ref, bias_got.at[k], b_send.at[k], b_recv.at[k], across(k))
    for j in (*range(1, chips), 0):
        start(
            grad_ref.at[part(1 - core, j)], pair_got.at[j], e_send.at[j], e_recv.at[j], sibling
        )
    for j in (*range(1, chips), 0):
        remote(
            grad_ref.at[part(1 - core, j)], pair_got.at[j], e_send.at[j], e_recv.at[j], sibling
        ).wait_recv()
        grad_sum = grad_ref[part(core, j), :] + pair_got[j]
        if j > 0:
            pair_sum[j] = grad_sum.astype(BF16)
            start(pair_sum.at[j], grad_got.at[j], g_send.at[j], g_recv.at[j], other_chip(j))
    for k in range(1, blocks):
        remote(
            pooled_in.at[0], pooled_got.at[k], p_send.at[k], p_recv.at[k], across(k)
        ).wait_recv()

    def select(j, carry):
        slot, found = 0, 0.0
        for k in range(blocks):
            hit = codes_ref[lax.rem(block + blocks - k, blocks), 0] == j
            slot = jnp.where(hit, k, slot)
            found = jnp.where(hit, 1.0, found)
        total = pooled_got[slot].astype(F32) * found
        pooled_sel[lax.div(j, work), lax.rem(j, work)] = total.astype(BF16)
        return carry

    lax.fori_loop(0, regions * work, select, 0)
    for k in range(1, regions):
        peer = lax.rem(region + k, regions)
        start(pooled_sel.at[peer], pooled_end.at[k], q_send.at[k], q_recv.at[k], along(k))
    bias_sum = bias_ref[...]
    for k in range(1, blocks):
        remote(bias_ref, bias_got.at[k], b_send.at[k], b_recv.at[k], across(k)).wait_recv()
        bias_sum = bias_sum + bias_got[k]
    bias_part[region] = bias_sum
    for k in range(1, regions):
        start(
            bias_part.at[region], bias_part.at[region], c_send.at[k], c_recv.at[k], along(k)
        )

    for j in range(1, chips):
        remote(
            pair_sum.at[j], grad_got.at[j], g_send.at[j], g_recv.at[j], other_chip(j)
        ).wait_recv()
        grad_sum = grad_sum + grad_got[j].astype(F32)
    grad_part[...] = grad_sum.reshape(grad_part.shape)
    for k in range(1, regions):
        peer = lax.rem(region + k, regions)
        start(grad_part.at[peer], grad_slice.at[k], h_send.at[k], h_recv.at[k], along(k))
    for k in range(1, regions):
        remote(
            grad_part.at[0], grad_slice.at[k], h_send.at[k], h_recv.at[k], along(k)
        ).wait_recv()
    grad_sum = grad_part[region]
    for k in range(1, regions):
        grad_sum = grad_sum + grad_slice[k]
    grad_full[region] = grad_sum
    for k in range(1, regions):
        start(
            grad_full.at[region], grad_full.at[region], d_send.at[k], d_recv.at[k], along(k)
        )
    for k in range(1, regions):
        source = lax.rem(region + regions - k, regions)
        remote(
            grad_full.at[source], grad_full.at[source], d_send.at[k], d_recv.at[k], along(k)
        ).wait_recv()
    grad_sum = grad_full[...].reshape(shard, -1)
    own = grad_all.at[core, chip]
    own[...] = grad_sum.astype(BF16)
    for j in range(1, chips):
        start(own, own, a_send.at[j], a_recv.at[j], other_chip(j))
    start(own, own, f_send.at[0], f_recv.at[0], sibling)
    for j in range(1, chips):
        slot = grad_all.at[core, lax.rem(chip + chips - j, chips)]
        remote(slot, slot, a_send.at[j], a_recv.at[j], other_chip(j)).wait_recv()
        start(slot, slot, f_send.at[j], f_recv.at[j], sibling)

    for k in range(1, regions):
        source = lax.rem(region + regions - k, regions)
        remote(
            bias_part.at[source], bias_part.at[source], c_send.at[k], c_recv.at[k], along(k)
        ).wait_recv()
        remote(
            pooled_sel.at[0], pooled_end.at[k], q_send.at[k], q_recv.at[k], along(k)
        ).wait_recv()
    bias_sum = bias_part[0]
    for r in range(1, regions):
        bias_sum = bias_sum + bias_part[r]
    bias_out[...] = bias_sum
    for s in range(work):
        rows = pooled_sel[region, s].astype(F32)
        for k in range(1, regions):
            rows = rows + pooled_end[k, s].astype(F32)
        width = rows.shape[1] // 2
        pooled_ref[s] = jnp.concatenate([rows[:, :width], rows[:, width:]], axis=0).astype(BF16)

    for j in range(chips):
        slot = grad_all.at[1 - core, lax.rem(chip + chips - j, chips)]
        remote(slot, slot, f_send.at[j], f_recv.at[j], sibling).wait_recv()
    rows_total = weight_out.shape[0]
    for w in range(blocks):
        low, high = w * shard, min((w + 1) * shard, rows_total)
        if low < high:
            weight_out[low:high, :] = grad_all[w // chips, w % chips, : high - low, :].astype(F32)
    for copy in sends:
        copy.wait_send()


def per_device(
    features,
    counts,
    rebalance,
    neighbors,
    coarse_owner,
    conv_weight,
    convolution_bias_vector,
    merged_adjoint,
):
    home, channels = features.shape[0], features.shape[1]
    taps, _, outs = conv_weight.shape
    work = home // 2
    regions, blocks = lax.axis_size("region"), lax.axis_size("block")
    cells = merged_adjoint.shape[1] // outs
    rows = taps * channels
    dense = (outs // 2, 2 * cells)
    chips = blocks // 2
    unit = math.lcm(16, 8 * regions)
    shard = -(-rows // (blocks * unit)) * unit
    vmem = pl.BlockSpec(memory_space=pltpu.VMEM)
    smem = pl.BlockSpec(memory_space=pltpu.SMEM)
    dma = pltpu.SemaphoreType.DMA
    shape = jax.ShapeDtypeStruct

    pooled, weight_total, bias_total = pl.pallas_call(
        functools.partial(fused_kernel, regions, blocks, shard),
        out_shape=(
            shape((work, outs, cells), BF16),
            shape((rows, outs), F32),
            shape((8, outs), F32),
        ),
        in_specs=[smem] * 4 + [vmem] * 4,
        out_specs=(vmem, vmem, vmem),
        scratch_shapes=[
            pltpu.VMEM((3, home, channels, 128), BF16),
            pltpu.VMEM((blocks,) + dense, BF16),
            pltpu.VMEM((blocks, 128), jnp.int32),
            pltpu.VMEM((blocks, blocks, 128), jnp.int32),
            pltpu.SMEM((blocks, 128), jnp.int32),
            pltpu.VMEM((regions * work,) + dense, BF16),
            pltpu.VMEM((blocks,) + dense, BF16),
            pltpu.VMEM((home + 1, channels, 512), F32),
            pltpu.VMEM((3 * home + 1, channels, 128), F32),
            pltpu.VMEM((home, rows, 512), BF16),
            pltpu.VMEM((home, outs, 512), F32),
            pltpu.VMEM((home,) + dense, BF16),
            pltpu.VMEM((blocks,) + dense, BF16),
            pltpu.VMEM((blocks * shard, outs), F32),
            pltpu.VMEM((8, outs), F32),
            pltpu.VMEM((blocks,) + dense, BF16),
            pltpu.VMEM((regions, work) + dense, BF16),
            pltpu.VMEM((regions, work) + dense, BF16),
            pltpu.VMEM((chips, shard, outs), F32),
            pltpu.VMEM((chips, shard, outs), BF16),
            pltpu.VMEM((chips, shard, outs), BF16),
            pltpu.VMEM((regions, shard // regions, outs), F32),
            pltpu.VMEM((regions, shard // regions, outs), F32),
            pltpu.VMEM((regions, shard // regions, outs), F32),
            pltpu.VMEM((2, chips, shard, outs), BF16),
            pltpu.VMEM((blocks, 8, outs), F32),
            pltpu.VMEM((regions, 8, outs), F32),
            dma,
            dma((2,)),
            dma((2,)),
        ]
        + [dma((regions,))] * 10
        + [dma((blocks,))] * 8
        + [dma((chips,))] * 8,
        compiler_params=pltpu.CompilerParams(
            collective_id=0, has_side_effects=True, vmem_limit_bytes=VMEM_LIMIT
        ),
        name="fused",
    )(
        counts,
        rebalance,
        coarse_owner,
        neighbors,
        features,
        merged_adjoint.reshape(work, outs, cells),
        conv_weight.reshape(rows, outs),
        convolution_bias_vector.reshape(outs, 1),
    )
    return (
        pooled.reshape(work, outs * cells),
        weight_total.reshape(taps, channels, outs),
        bias_total[0],
    )


def solution(mesh):
    in_specs = (
        P(("region", "block"), None, None),
        P(("region", "block")),
        P(("region", "block")),
        P(("region", "block"), None),
        P(("region", "block")),
        P(),
        P(),
        P(("region", "block"), None),
    )
    out_specs = (P(("region", "block"), None), P(), P())
    return jax.shard_map(
        per_device, mesh=mesh, in_specs=in_specs, out_specs=out_specs, check_vma=False
    )
```

```python
import functools
import math

import jax
import jax.numpy as jnp
from jax import lax
from jax.experimental import pallas as pl
from jax.experimental.pallas import tpu as pltpu
from jax.sharding import PartitionSpec as P

MESH = pl.DeviceIdType.MESH
VMEM_LIMIT = 48 * 1024 * 1024
F32 = jnp.float32
BF16 = jnp.bfloat16


def greet(region, block, regions, blocks):
    barrier = pltpu.get_barrier_semaphore()
    for k in range(1, blocks):
        pl.semaphore_signal(
            barrier, inc=1, device_id=(region, lax.rem(block + k, blocks)), device_id_type=MESH
        )
    for k in range(1, regions):
        pl.semaphore_signal(
            barrier, inc=1, device_id=(lax.rem(region + k, regions), block), device_id_type=MESH
        )
    pl.semaphore_wait(barrier, blocks + regions - 2)


def remote(src, dst, send_sem, recv_sem, device):
    return pltpu.make_async_remote_copy(
        src_ref=src,
        dst_ref=dst,
        send_sem=send_sem,
        recv_sem=recv_sem,
        device_id=device,
        device_id_type=MESH,
    )


def column(ea, eb, ec):
    t = 9 * (ea + 1) + 3 * (eb + 1) + (ec + 1)
    return t if t < 13 else t - 1


def fused_kernel(
    regions,
    blocks,
    shard,
    counts_ref,
    rebalance_ref,
    owner_ref,
    neighbors_ref,
    features_ref,
    adjoint_ref,
    weight_hbm,
    conv_bias_ref,
    pooled_ref,
    weight_out,
    bias_out,
    weight_ref,
    grads,
    layers_ref,
    cotangent_ref,
    mine_ref,
    tags_ref,
    codes_ref,
    adjoints,
    outgoing,
    cubes,
    slabs,
    stacked,
    preacts,
    pooled_block,
    pooled_in,
    grad_ref,
    bias_ref,
    pooled_got,
    pooled_sel,
    pooled_end,
    pair_got,
    pair_sum,
    grad_got,
    grad_part,
    grad_slice,
    grad_full,
    grad_all,
    bias_got,
    bias_part,
    weight_sem,
    code_sem,
    lay_send,
    lay_recv,
    adj_send,
    adj_recv,
    q_send,
    q_recv,
    h_send,
    h_recv,
    d_send,
    d_recv,
    c_send,
    c_recv,
    tag_send,
    tag_recv,
    cot_send,
    cot_recv,
    p_send,
    p_recv,
    b_send,
    b_recv,
    e_send,
    e_recv,
    f_send,
    f_recv,
    g_send,
    g_recv,
    a_send,
    a_recv,
):
    weight_copy = pltpu.make_async_copy(weight_hbm, weight_ref, weight_sem)
    weight_copy.start()
    region, block = lax.axis_index("region"), lax.axis_index("block")
    home = features_ref.shape[0]
    work = adjoint_ref.shape[0]
    rows = lax.broadcasted_iota(jnp.int32, (blocks, 128), 0)
    codes = jnp.full((blocks, 128), -1, jnp.int32)
    for h in range(home):
        line = rebalance_ref[h]
        device = jnp.where(line >= 0, lax.rem(lax.div(line, work), blocks), -1)
        code = owner_ref[h] * work + lax.rem(line, work)
        codes = jnp.where(rows == device, code, codes)
    tags_ref[block] = codes
    lanes = lax.broadcasted_iota(jnp.int32, (1, 64), 1)
    for h in range(home):
        for side, start in enumerate((0, 448)):
            live = (((lanes + start) * 167) & 511) < counts_ref[h]
            values = features_ref[h, :, start : start + 64].astype(F32)
            layers_ref[1, h, :, side * 64 : side * 64 + 64] = jnp.where(live, values, 0.0).astype(
                BF16
            )
    outs = adjoint_ref.shape[1] // 2
    for s in range(work):
        row = adjoint_ref[s].astype(F32)
        adjoints[region * work + s] = jnp.concatenate([row[:outs], row[outs:]], axis=1).astype(BF16)
    greet(region, block, regions, blocks)

    before = lax.rem(block + blocks - 1, blocks)
    after = lax.rem(block + 1, blocks)
    sends = []

    def start(*args):
        copy = remote(*args)
        copy.start()
        sends.append(copy)

    def across(k):
        return (region, lax.rem(block + k, blocks))

    def along(k):
        return (lax.rem(region + k, regions), block)

    core, chip, chips = lax.rem(block, 2), lax.div(block, 2), blocks // 2
    sibling = (region, block + 1 - 2 * core)

    def part(side, j):
        index = side * chips + lax.rem(chip + j, chips)
        return pl.ds(pl.multiple_of(index * shard, 16), shard)

    def other_chip(j):
        return (region, 2 * lax.rem(chip + j, chips) + core)

    for k in range(1, regions):
        copy = remote(
            adjoints.at[pl.ds(region * work, work)],
            adjoints.at[pl.ds(region * work, work)],
            adj_send.at[k],
            adj_recv.at[k],
            (lax.rem(region + k, regions), block),
        )
        copy.start()
        sends.append(copy)
    for k in range(1, blocks):
        copy = remote(
            tags_ref.at[block],
            tags_ref.at[block],
            tag_send.at[k],
            tag_recv.at[k],
            (region, lax.rem(block + k, blocks)),
        )
        copy.start()
        sends.append(copy)
    for i, (slot, target) in enumerate(((2, before), (0, after))):
        copy = remote(
            layers_ref.at[1], layers_ref.at[slot], lay_send.at[i], lay_recv.at[i], (region, target)
        )
        copy.start()
        sends.append(copy)
    for i, (slot, target) in enumerate(((2, after), (0, before))):
        remote(
            layers_ref.at[1], layers_ref.at[slot], lay_send.at[i], lay_recv.at[i], (region, target)
        ).wait_recv()
    channels = features_ref.shape[1]
    first = (region * blocks + block) * home
    voxel = lax.broadcasted_iota(jnp.int32, (1, 512), 1)
    hashed = (voxel * 167) & 511
    for h in range(home):
        cubes[h] = jnp.where(hashed < counts_ref[h], features_ref[h].astype(F32), 0.0)
        for d in range(3):
            slabs[d * home + h] = layers_ref[d, h].astype(F32)
    cubes[home] = jnp.zeros(cubes.shape[1:], F32)
    slabs[3 * home] = jnp.zeros(slabs.shape[1:], F32)
    used = weight_ref.shape[0]
    if stacked.shape[1] > used:
        for h in range(home):
            stacked[h, used:, :] = jnp.zeros((stacked.shape[1] - used, 512), BF16)
    bias_ref[...] = jnp.zeros_like(bias_ref)

    v = lax.broadcasted_iota(jnp.int32, (512, 64), 0)
    cell = ((v >> 7) * 4 + ((v >> 4) & 3)) * 4 + ((v & 7) >> 1)
    table = jnp.where(
        cell == lax.broadcasted_iota(jnp.int32, (512, 64), 1), 0.125, 0.0
    ).astype(BF16)
    lane = lax.broadcasted_iota(jnp.int32, (1, 640), 1)
    b_at, c_at = (lane >> 3) & 7, lane & 7
    half = lax.broadcasted_iota(jnp.int32, (1, 128), 1) < 64

    def shifted(x, offset):
        return pltpu.roll(x, (-offset) % 640, 1)

    def forward(g, carry):
        def slab(ea, fb, fc):
            target = neighbors_ref[g, column(ea, fb, fc)]
            return slabs[jnp.where(target >= 0, jnp.clip(target - (first - home), 0, 3 * home - 1), 3 * home)]

        def extended(fb, fc):
            if (fb, fc) == (0, 0):
                middle = cubes[g]
            else:
                target = neighbors_ref[g, column(0, fb, fc)]
                middle = cubes[jnp.where(target >= 0, jnp.clip(target - first, 0, home - 1), home)]
            ends = jnp.where(half, slab(1, fb, fc), slab(-1, fb, fc))
            return jnp.concatenate([middle, ends], axis=1)

        for ec in (-1, 0, 1):
            along = {}
            for fb in (-1, 0, 1):
                if ec == 0:
                    along[fb] = extended(fb, 0)
                else:
                    out = (c_at + ec) != ((c_at + ec) & 7)
                    along[fb] = jnp.where(
                        out,
                        shifted(extended(fb, ec), -7 * ec),
                        shifted(extended(fb, 0), ec),
                    )
            for eb in (-1, 0, 1):
                if eb == 0:
                    plane = along[0]
                else:
                    out = (b_at + eb) != ((b_at + eb) & 7)
                    plane = jnp.where(
                        out, shifted(along[eb], -56 * eb), shifted(along[0], 8 * eb)
                    )
                for ea in (-1, 0, 1):
                    tap = 9 * (ea + 1) + 3 * (eb + 1) + (ec + 1)
                    moved = plane if ea == 0 else shifted(plane, 64 * ea)
                    stacked[g, tap * channels : (tap + 1) * channels, :] = moved[:, :512].astype(BF16)

        preact = (
            lax.dot_general(
                weight_ref[...],
                stacked[g, :used, :],
                (((0,), (0,)), ((), ())),
                preferred_element_type=F32,
            )
            + conv_bias_ref[...]
        )
        live = hashed < counts_ref[g]
        gate = jax.nn.sigmoid(preact)
        active = jnp.where(live, preact * gate, 0.0)
        high = active.astype(BF16)
        low = (active - high.astype(F32)).astype(BF16)
        pooled = jnp.dot(high, table, preferred_element_type=F32) + jnp.dot(
            low, table, preferred_element_type=F32
        )
        middle = pooled.shape[0] // 2
        pooled_block[g] = jnp.concatenate([pooled[:middle], pooled[middle:]], axis=1).astype(
            BF16
        )
        preacts[g] = preact
        return carry

    weight_copy.wait()
    lax.fori_loop(0, 1, forward, 0)
    for k in range(1, blocks):
        source = lax.rem(block + blocks - k, blocks)
        remote(
            tags_ref.at[source],
            tags_ref.at[source],
            tag_send.at[k],
            tag_recv.at[k],
            (region, source),
        ).wait_recv()
        mine_ref[pl.ds(source, 1), :] = tags_ref[source, pl.ds(block, 1), :]
    mine_ref[pl.ds(block, 1), :] = tags_ref[block, pl.ds(block, 1), :]
    codes_copy = pltpu.make_async_copy(mine_ref, codes_ref, code_sem)
    codes_copy.start()
    codes_copy.wait()
    for k in range(1, regions):
        source = lax.rem(region + regions - k, regions)
        remote(
            adjoints.at[pl.ds(source * work, work)],
            adjoints.at[pl.ds(source * work, work)],
            adj_send.at[k],
            adj_recv.at[k],
            (source, block),
        ).wait_recv()
    for k in range(1, blocks):
        source = lax.rem(block + blocks - k, blocks)
        outgoing[source] = adjoints[jnp.clip(codes_ref[source, 0], 0, regions * work - 1)]
        copy = remote(
            outgoing.at[source],
            cotangent_ref.at[block],
            cot_send.at[blocks - k],
            cot_recv.at[blocks - k],
            (region, source),
        )
        copy.start()
        sends.append(copy)
    cotangent_ref[block] = adjoints[jnp.clip(codes_ref[block, 0], 0, regions * work - 1)]
    lax.fori_loop(1, home, forward, 0)
    for w in range(blocks):
        slot = 0
        for h in range(home):
            line = rebalance_ref[h]
            hit = (line >= 0) & (lax.rem(lax.div(line, work), blocks) == w)
            slot = jnp.where(hit, h, slot)
        pooled_in[w] = pooled_block[slot]
    for k in range(1, blocks):
        peer = lax.rem(block + k, blocks)
        start(pooled_in.at[peer], pooled_got.at[k], p_send.at[k], p_recv.at[k], across(k))
    pooled_got[0] = pooled_in[block]
    for k in range(1, blocks):
        source = lax.rem(block + blocks - k, blocks)
        remote(
            outgoing.at[source],
            cotangent_ref.at[source],
            cot_send.at[k],
            cot_recv.at[k],
            (region, source),
        ).wait_recv()

    def backward(g, carry):
        preact = preacts[g]
        live = hashed < counts_ref[g]
        gate = jax.nn.sigmoid(preact)
        line = jnp.maximum(rebalance_ref[g], 0)
        device = lax.rem(lax.div(line, work), blocks)
        row = cotangent_ref[device].astype(F32)
        width = row.shape[1] // 2
        row = jnp.concatenate([row[:, :width], row[:, width:]], axis=0).astype(BF16)
        spread = lax.dot_general(
            row,
            table,
            (((1,), (1,)), ((), ())),
            preferred_element_type=F32,
        )
        grad = jnp.where(live, spread * gate * (1.0 + preact * (1.0 - gate)), 0.0)
        grad_high = grad.astype(BF16)
        grad_low = (grad - grad_high.astype(F32)).astype(BF16)
        grads[g] = grad_high
        ones = jnp.ones((8, 512), BF16)
        for part in (grad_high, grad_low):
            bias_ref[...] += lax.dot_general(
                ones, part, (((1,), (1,)), ((), ())), preferred_element_type=F32
            )
        return carry

    lax.fori_loop(0, home, backward, 0)
    for k in range(1, blocks):
        start(bias_ref, bias_got.at[k], b_send.at[k], b_recv.at[k], across(k))

    def slice_of(side, j):
        rows = part(side, j)
        total = jnp.zeros((shard, grad_ref.shape[1]), F32)
        for h in range(home):
            total = total + lax.dot_general(
                stacked[h, rows, :],
                grads[h],
                (((1,), (1,)), ((), ())),
                preferred_element_type=F32,
            )
        return total

    for j in (*range(1, chips), 0):
        grad_ref[part(1 - core, j), :] = slice_of(1 - core, j)
        start(
            grad_ref.at[part(1 - core, j)], pair_got.at[j], e_send.at[j], e_recv.at[j], sibling
        )
    for j in (*range(1, chips), 0):
        grad_sum = slice_of(core, j)
        remote(
            grad_ref.at[part(1 - core, j)], pair_got.at[j], e_send.at[j], e_recv.at[j], sibling
        ).wait_recv()
        grad_sum = grad_sum + pair_got[j]
        if j > 0:
            pair_sum[j] = grad_sum.astype(BF16)
            start(pair_sum.at[j], grad_got.at[j], g_send.at[j], g_recv.at[j], other_chip(j))
    for k in range(1, blocks):
        remote(
            pooled_in.at[0], pooled_got.at[k], p_send.at[k], p_recv.at[k], across(k)
        ).wait_recv()

    def select(j, carry):
        slot, found = 0, 0.0
        for k in range(blocks):
            hit = codes_ref[lax.rem(block + blocks - k, blocks), 0] == j
            slot = jnp.where(hit, k, slot)
            found = jnp.where(hit, 1.0, found)
        total = pooled_got[slot].astype(F32) * found
        pooled_sel[lax.div(j, work), lax.rem(j, work)] = total.astype(BF16)
        return carry

    lax.fori_loop(0, regions * work, select, 0)
    for k in range(1, regions):
        peer = lax.rem(region + k, regions)
        start(pooled_sel.at[peer], pooled_end.at[k], q_send.at[k], q_recv.at[k], along(k))
    bias_sum = bias_ref[...]
    for k in range(1, blocks):
        remote(bias_ref, bias_got.at[k], b_send.at[k], b_recv.at[k], across(k)).wait_recv()
        bias_sum = bias_sum + bias_got[k]
    bias_part[region] = bias_sum
    for k in range(1, regions):
        start(
            bias_part.at[region], bias_part.at[region], c_send.at[k], c_recv.at[k], along(k)
        )

    for j in range(1, chips):
        remote(
            pair_sum.at[j], grad_got.at[j], g_send.at[j], g_recv.at[j], other_chip(j)
        ).wait_recv()
        grad_sum = grad_sum + grad_got[j].astype(F32)
    grad_part[...] = grad_sum.reshape(grad_part.shape)
    for k in range(1, regions):
        peer = lax.rem(region + k, regions)
        start(grad_part.at[peer], grad_slice.at[k], h_send.at[k], h_recv.at[k], along(k))
    for k in range(1, regions):
        remote(
            grad_part.at[0], grad_slice.at[k], h_send.at[k], h_recv.at[k], along(k)
        ).wait_recv()
    grad_sum = grad_part[region]
    for k in range(1, regions):
        grad_sum = grad_sum + grad_slice[k]
    grad_full[region] = grad_sum
    for k in range(1, regions):
        start(
            grad_full.at[region], grad_full.at[region], d_send.at[k], d_recv.at[k], along(k)
        )
    for k in range(1, regions):
        source = lax.rem(region + regions - k, regions)
        remote(
            grad_full.at[source], grad_full.at[source], d_send.at[k], d_recv.at[k], along(k)
        ).wait_recv()
    grad_sum = grad_full[...].reshape(shard, -1)
    own = grad_all.at[core, chip]
    own[...] = grad_sum.astype(BF16)
    for j in range(1, chips):
        start(own, own, a_send.at[j], a_recv.at[j], other_chip(j))
    start(own, own, f_send.at[0], f_recv.at[0], sibling)
    for j in range(1, chips):
        slot = grad_all.at[core, lax.rem(chip + chips - j, chips)]
        remote(slot, slot, a_send.at[j], a_recv.at[j], other_chip(j)).wait_recv()
        start(slot, slot, f_send.at[j], f_recv.at[j], sibling)

    for k in range(1, regions):
        source = lax.rem(region + regions - k, regions)
        remote(
            bias_part.at[source], bias_part.at[source], c_send.at[k], c_recv.at[k], along(k)
        ).wait_recv()
        remote(
            pooled_sel.at[0], pooled_end.at[k], q_send.at[k], q_recv.at[k], along(k)
        ).wait_recv()
    bias_sum = bias_part[0]
    for r in range(1, regions):
        bias_sum = bias_sum + bias_part[r]
    bias_out[...] = bias_sum
    for s in range(work):
        rows = pooled_sel[region, s].astype(F32)
        for k in range(1, regions):
            rows = rows + pooled_end[k, s].astype(F32)
        width = rows.shape[1] // 2
        pooled_ref[s] = jnp.concatenate([rows[:, :width], rows[:, width:]], axis=0).astype(BF16)

    for j in range(chips):
        slot = grad_all.at[1 - core, lax.rem(chip + chips - j, chips)]
        remote(slot, slot, f_send.at[j], f_recv.at[j], sibling).wait_recv()
    rows_total = weight_out.shape[0]
    for w in range(blocks):
        low, high = w * shard, min((w + 1) * shard, rows_total)
        if low < high:
            weight_out[low:high, :] = grad_all[w // chips, w % chips, : high - low, :].astype(F32)
    for copy in sends:
        copy.wait_send()


def per_device(
    features,
    counts,
    rebalance,
    neighbors,
    coarse_owner,
    conv_weight,
    convolution_bias_vector,
    merged_adjoint,
):
    home, channels = features.shape[0], features.shape[1]
    taps, _, outs = conv_weight.shape
    work = home // 2
    regions, blocks = lax.axis_size("region"), lax.axis_size("block")
    cells = merged_adjoint.shape[1] // outs
    rows = taps * channels
    dense = (outs // 2, 2 * cells)
    chips = blocks // 2
    unit = math.lcm(16, 8 * regions)
    shard = -(-rows // (blocks * unit)) * unit
    vmem = pl.BlockSpec(memory_space=pltpu.VMEM)
    smem = pl.BlockSpec(memory_space=pltpu.SMEM)
    dma = pltpu.SemaphoreType.DMA
    shape = jax.ShapeDtypeStruct

    pooled, weight_total, bias_total = pl.pallas_call(
        functools.partial(fused_kernel, regions, blocks, shard),
        out_shape=(
            shape((work, outs, cells), BF16),
            shape((rows, outs), F32),
            shape((8, outs), F32),
        ),
        in_specs=[smem] * 4 + [vmem, vmem, pl.BlockSpec(memory_space=pl.ANY), vmem],
        out_specs=(vmem, vmem, vmem),
        scratch_shapes=[
            pltpu.VMEM((rows, outs), BF16),
            pltpu.VMEM((home, outs, 512), BF16),
            pltpu.VMEM((3, home, channels, 128), BF16),
            pltpu.VMEM((blocks,) + dense, BF16),
            pltpu.VMEM((blocks, 128), jnp.int32),
            pltpu.VMEM((blocks, blocks, 128), jnp.int32),
            pltpu.SMEM((blocks, 128), jnp.int32),
            pltpu.VMEM((regions * work,) + dense, BF16),
            pltpu.VMEM((blocks,) + dense, BF16),
            pltpu.VMEM((home + 1, channels, 512), F32),
            pltpu.VMEM((3 * home + 1, channels, 128), F32),
            pltpu.VMEM((home, blocks * shard, 512), BF16),
            pltpu.VMEM((home, outs, 512), F32),
            pltpu.VMEM((home,) + dense, BF16),
            pltpu.VMEM((blocks,) + dense, BF16),
            pltpu.VMEM((blocks * shard, outs), F32),
            pltpu.VMEM((8, outs), F32),
            pltpu.VMEM((blocks,) + dense, BF16),
            pltpu.VMEM((regions, work) + dense, BF16),
            pltpu.VMEM((regions, work) + dense, BF16),
            pltpu.VMEM((chips, shard, outs), F32),
            pltpu.VMEM((chips, shard, outs), BF16),
            pltpu.VMEM((chips, shard, outs), BF16),
            pltpu.VMEM((regions, shard // regions, outs), F32),
            pltpu.VMEM((regions, shard // regions, outs), F32),
            pltpu.VMEM((regions, shard // regions, outs), F32),
            pltpu.VMEM((2, chips, shard, outs), BF16),
            pltpu.VMEM((blocks, 8, outs), F32),
            pltpu.VMEM((regions, 8, outs), F32),
            dma,
            dma,
            dma((2,)),
            dma((2,)),
        ]
        + [dma((regions,))] * 10
        + [dma((blocks,))] * 8
        + [dma((chips,))] * 8,
        compiler_params=pltpu.CompilerParams(
            collective_id=0, has_side_effects=True, vmem_limit_bytes=VMEM_LIMIT
        ),
        name="fused",
    )(
        counts,
        rebalance,
        coarse_owner,
        neighbors,
        features,
        merged_adjoint.reshape(work, outs, cells),
        conv_weight.reshape(rows, outs),
        convolution_bias_vector.reshape(outs, 1),
    )
    return (
        pooled.reshape(work, outs * cells),
        weight_total.reshape(taps, channels, outs),
        bias_total[0],
    )


def solution(mesh):
    in_specs = (
        P(("region", "block"), None, None),
        P(("region", "block")),
        P(("region", "block")),
        P(("region", "block"), None),
        P(("region", "block")),
        P(),
        P(),
        P(("region", "block"), None),
    )
    out_specs = (P(("region", "block"), None), P(), P())
    return jax.shard_map(
        per_device, mesh=mesh, in_specs=in_specs, out_specs=out_specs, check_vma=False
    )
```

```python
import functools
import math

import jax
import jax.numpy as jnp
from jax import lax
from jax.experimental import pallas as pl
from jax.experimental.pallas import tpu as pltpu
from jax.sharding import PartitionSpec as P

MESH = pl.DeviceIdType.MESH
VMEM_LIMIT = 48 * 1024 * 1024
F32 = jnp.float32
BF16 = jnp.bfloat16


def greet(region, block, regions, blocks):
    barrier = pltpu.get_barrier_semaphore()
    for k in range(1, blocks):
        pl.semaphore_signal(
            barrier, inc=1, device_id=(region, lax.rem(block + k, blocks)), device_id_type=MESH
        )
    for k in range(1, regions):
        pl.semaphore_signal(
            barrier, inc=1, device_id=(lax.rem(region + k, regions), block), device_id_type=MESH
        )
    pl.semaphore_wait(barrier, blocks + regions - 2)


def remote(src, dst, send_sem, recv_sem, device):
    return pltpu.make_async_remote_copy(
        src_ref=src,
        dst_ref=dst,
        send_sem=send_sem,
        recv_sem=recv_sem,
        device_id=device,
        device_id_type=MESH,
    )


def column(ea, eb, ec):
    t = 9 * (ea + 1) + 3 * (eb + 1) + (ec + 1)
    return t if t < 13 else t - 1


def fused_kernel(
    regions,
    blocks,
    shard,
    counts_ref,
    rebalance_ref,
    owner_ref,
    neighbors_ref,
    features_ref,
    adjoint_ref,
    weight_ref,
    conv_bias_ref,
    pooled_ref,
    weight_out,
    bias_out,
    layers_ref,
    cotangent_ref,
    mine_ref,
    tags_ref,
    codes_ref,
    adjoints,
    outgoing,
    cubes,
    slabs,
    stacked,
    preacts,
    pooled_block,
    pooled_in,
    grad_ref,
    bias_ref,
    pooled_got,
    pooled_sel,
    pooled_end,
    pair_got,
    pair_sum,
    grad_got,
    grad_part,
    grad_slice,
    grad_full,
    grad_all,
    bias_got,
    bias_part,
    code_sem,
    lay_send,
    lay_recv,
    adj_send,
    adj_recv,
    q_send,
    q_recv,
    h_send,
    h_recv,
    d_send,
    d_recv,
    c_send,
    c_recv,
    tag_send,
    tag_recv,
    cot_send,
    cot_recv,
    p_send,
    p_recv,
    b_send,
    b_recv,
    e_send,
    e_recv,
    f_send,
    f_recv,
    g_send,
    g_recv,
    a_send,
    a_recv,
):
    region, block = lax.axis_index("region"), lax.axis_index("block")
    home = features_ref.shape[0]
    work = adjoint_ref.shape[0]
    rows = lax.broadcasted_iota(jnp.int32, (blocks, 128), 0)
    codes = jnp.full((blocks, 128), -1, jnp.int32)
    for h in range(home):
        line = rebalance_ref[h]
        device = jnp.where(line >= 0, lax.rem(lax.div(line, work), blocks), -1)
        code = owner_ref[h] * work + lax.rem(line, work)
        codes = jnp.where(rows == device, code, codes)
    tags_ref[block] = codes
    lanes = lax.broadcasted_iota(jnp.int32, (1, 64), 1)
    for h in range(home):
        for side, start in enumerate((0, 448)):
            live = (((lanes + start) * 167) & 511) < counts_ref[h]
            values = features_ref[h, :, start : start + 64].astype(F32)
            layers_ref[1, h, :, side * 64 : side * 64 + 64] = jnp.where(live, values, 0.0).astype(
                BF16
            )
    outs = adjoint_ref.shape[1] // 2
    for s in range(work):
        row = adjoint_ref[s].astype(F32)
        adjoints[region * work + s] = jnp.concatenate([row[:outs], row[outs:]], axis=1).astype(BF16)
    greet(region, block, regions, blocks)

    before = lax.rem(block + blocks - 1, blocks)
    after = lax.rem(block + 1, blocks)
    sends = []

    def start(*args):
        copy = remote(*args)
        copy.start()
        sends.append(copy)

    def across(k):
        return (region, lax.rem(block + k, blocks))

    def along(k):
        return (lax.rem(region + k, regions), block)

    core, chip, chips = lax.rem(block, 2), lax.div(block, 2), blocks // 2
    sibling = (region, block + 1 - 2 * core)

    def part(side, j):
        index = side * chips + lax.rem(chip + j, chips)
        return pl.ds(pl.multiple_of(index * shard, 16), shard)

    def other_chip(j):
        return (region, 2 * lax.rem(chip + j, chips) + core)

    for k in range(1, regions):
        copy = remote(
            adjoints.at[pl.ds(region * work, work)],
            adjoints.at[pl.ds(region * work, work)],
            adj_send.at[k],
            adj_recv.at[k],
            (lax.rem(region + k, regions), block),
        )
        copy.start()
        sends.append(copy)
    for k in range(1, blocks):
        copy = remote(
            tags_ref.at[block],
            tags_ref.at[block],
            tag_send.at[k],
            tag_recv.at[k],
            (region, lax.rem(block + k, blocks)),
        )
        copy.start()
        sends.append(copy)
    for i, (slot, target) in enumerate(((2, before), (0, after))):
        copy = remote(
            layers_ref.at[1], layers_ref.at[slot], lay_send.at[i], lay_recv.at[i], (region, target)
        )
        copy.start()
        sends.append(copy)
    for k in range(1, blocks):
        source = lax.rem(block + blocks - k, blocks)
        remote(
            tags_ref.at[source],
            tags_ref.at[source],
            tag_send.at[k],
            tag_recv.at[k],
            (region, source),
        ).wait_recv()
        mine_ref[pl.ds(source, 1), :] = tags_ref[source, pl.ds(block, 1), :]
    mine_ref[pl.ds(block, 1), :] = tags_ref[block, pl.ds(block, 1), :]
    codes_copy = pltpu.make_async_copy(mine_ref, codes_ref, code_sem)
    codes_copy.start()
    codes_copy.wait()
    for k in range(1, regions):
        source = lax.rem(region + regions - k, regions)
        remote(
            adjoints.at[pl.ds(source * work, work)],
            adjoints.at[pl.ds(source * work, work)],
            adj_send.at[k],
            adj_recv.at[k],
            (source, block),
        ).wait_recv()
    for k in range(1, blocks):
        source = lax.rem(block + blocks - k, blocks)
        outgoing[source] = adjoints[jnp.clip(codes_ref[source, 0], 0, regions * work - 1)]
        copy = remote(
            outgoing.at[source],
            cotangent_ref.at[block],
            cot_send.at[blocks - k],
            cot_recv.at[blocks - k],
            (region, source),
        )
        copy.start()
        sends.append(copy)
    cotangent_ref[block] = adjoints[jnp.clip(codes_ref[block, 0], 0, regions * work - 1)]
    for i, (slot, target) in enumerate(((2, after), (0, before))):
        remote(
            layers_ref.at[1], layers_ref.at[slot], lay_send.at[i], lay_recv.at[i], (region, target)
        ).wait_recv()
    channels = features_ref.shape[1]
    first = (region * blocks + block) * home
    voxel = lax.broadcasted_iota(jnp.int32, (1, 512), 1)
    hashed = (voxel * 167) & 511
    for h in range(home):
        cubes[h] = jnp.where(hashed < counts_ref[h], features_ref[h].astype(F32), 0.0)
        for d in range(3):
            slabs[d * home + h] = layers_ref[d, h].astype(F32)
    cubes[home] = jnp.zeros(cubes.shape[1:], F32)
    slabs[3 * home] = jnp.zeros(slabs.shape[1:], F32)
    used = weight_ref.shape[0]
    grad_ref[...] = jnp.zeros_like(grad_ref)
    bias_ref[...] = jnp.zeros_like(bias_ref)

    v = lax.broadcasted_iota(jnp.int32, (512, 64), 0)
    cell = ((v >> 7) * 4 + ((v >> 4) & 3)) * 4 + ((v & 7) >> 1)
    table = jnp.where(
        cell == lax.broadcasted_iota(jnp.int32, (512, 64), 1), 0.125, 0.0
    ).astype(BF16)
    lane = lax.broadcasted_iota(jnp.int32, (1, 640), 1)
    b_at, c_at = (lane >> 3) & 7, lane & 7
    half = lax.broadcasted_iota(jnp.int32, (1, 128), 1) < 64

    def shifted(x, offset):
        return pltpu.roll(x, (-offset) % 640, 1)

    outs = conv_bias_ref.shape[1]
    diagonal = lax.broadcasted_iota(jnp.int32, (outs, outs), 0) == lax.broadcasted_iota(
        jnp.int32, (outs, outs), 1
    )
    bias_column = jnp.sum(
        jnp.where(diagonal, conv_bias_ref[...], 0.0), axis=1, keepdims=True
    )

    def forward(g, carry):
        def slab(ea, fb, fc):
            target = neighbors_ref[g, column(ea, fb, fc)]
            return slabs[jnp.where(target >= 0, jnp.clip(target - (first - home), 0, 3 * home - 1), 3 * home)]

        def extended(fb, fc):
            if (fb, fc) == (0, 0):
                middle = cubes[g]
            else:
                target = neighbors_ref[g, column(0, fb, fc)]
                middle = cubes[jnp.where(target >= 0, jnp.clip(target - first, 0, home - 1), home)]
            ends = jnp.where(half, slab(1, fb, fc), slab(-1, fb, fc))
            return jnp.concatenate([middle, ends], axis=1)

        for ec in (-1, 0, 1):
            along = {}
            for fb in (-1, 0, 1):
                if ec == 0:
                    along[fb] = extended(fb, 0)
                else:
                    out = (c_at + ec) != ((c_at + ec) & 7)
                    along[fb] = jnp.where(
                        out,
                        shifted(extended(fb, ec), -7 * ec),
                        shifted(extended(fb, 0), ec),
                    )
            for eb in (-1, 0, 1):
                if eb == 0:
                    plane = along[0]
                else:
                    out = (b_at + eb) != ((b_at + eb) & 7)
                    plane = jnp.where(
                        out, shifted(along[eb], -56 * eb), shifted(along[0], 8 * eb)
                    )
                for ea in (-1, 0, 1):
                    tap = 9 * (ea + 1) + 3 * (eb + 1) + (ec + 1)
                    moved = plane if ea == 0 else shifted(plane, 64 * ea)
                    stacked[g, tap * channels : (tap + 1) * channels, :] = moved[:, :512].astype(BF16)

        preact = (
            lax.dot_general(
                weight_ref[...],
                stacked[g],
                (((0,), (0,)), ((), ())),
                preferred_element_type=F32,
            )
            + bias_column
        )
        live = hashed < counts_ref[g]
        gate = jax.nn.sigmoid(preact)
        active = jnp.where(live, preact * gate, 0.0)
        high = active.astype(BF16)
        low = (active - high.astype(F32)).astype(BF16)
        pooled = jnp.dot(high, table, preferred_element_type=F32) + jnp.dot(
            low, table, preferred_element_type=F32
        )
        middle = pooled.shape[0] // 2
        pooled_block[g] = jnp.concatenate([pooled[:middle], pooled[middle:]], axis=1).astype(
            BF16
        )
        preacts[g] = preact
        return carry

    lax.fori_loop(0, home, forward, 0)
    for w in range(blocks):
        slot = 0
        for h in range(home):
            line = rebalance_ref[h]
            hit = (line >= 0) & (lax.rem(lax.div(line, work), blocks) == w)
            slot = jnp.where(hit, h, slot)
        pooled_in[w] = pooled_block[slot]
    for k in range(1, blocks):
        peer = lax.rem(block + k, blocks)
        start(pooled_in.at[peer], pooled_got.at[k], p_send.at[k], p_recv.at[k], across(k))
    pooled_got[0] = pooled_in[block]
    for k in range(1, blocks):
        source = lax.rem(block + blocks - k, blocks)
        remote(
            outgoing.at[source],
            cotangent_ref.at[source],
            cot_send.at[k],
            cot_recv.at[k],
            (region, source),
        ).wait_recv()

    def backward(g, carry):
        preact = preacts[g]
        live = hashed < counts_ref[g]
        gate = jax.nn.sigmoid(preact)
        line = jnp.maximum(rebalance_ref[g], 0)
        device = lax.rem(lax.div(line, work), blocks)
        row = cotangent_ref[device].astype(F32)
        width = row.shape[1] // 2
        row = jnp.concatenate([row[:, :width], row[:, width:]], axis=0).astype(BF16)
        spread = lax.dot_general(
            row,
            table,
            (((1,), (1,)), ((), ())),
            preferred_element_type=F32,
        )
        grad = jnp.where(live, spread * gate * (1.0 + preact * (1.0 - gate)), 0.0)
        grad_high = grad.astype(BF16)
        grad_low = (grad - grad_high.astype(F32)).astype(BF16)
        grad_ref[:used, :] += lax.dot_general(
            stacked[g], grad_high, (((1,), (1,)), ((), ())), preferred_element_type=F32
        )
        ones = jnp.ones((8, 512), BF16)
        for part in (grad_high, grad_low):
            bias_ref[...] += lax.dot_general(
                ones, part, (((1,), (1,)), ((), ())), preferred_element_type=F32
            )
        return carry

    lax.fori_loop(0, home, backward, 0)
    for k in range(1, blocks):
        start(bias_ref, bias_got.at[k], b_send.at[k], b_recv.at[k], across(k))
    for j in (*range(1, chips), 0):
        start(
            grad_ref.at[part(1 - core, j)], pair_got.at[j], e_send.at[j], e_recv.at[j], sibling
        )
    for j in (*range(1, chips), 0):
        remote(
            grad_ref.at[part(1 - core, j)], pair_got.at[j], e_send.at[j], e_recv.at[j], sibling
        ).wait_recv()
        grad_sum = grad_ref[part(core, j), :] + pair_got[j]
        if j > 0:
            pair_sum[j] = grad_sum.astype(BF16)
            start(pair_sum.at[j], grad_got.at[j], g_send.at[j], g_recv.at[j], other_chip(j))
    for k in range(1, blocks):
        remote(
            pooled_in.at[0], pooled_got.at[k], p_send.at[k], p_recv.at[k], across(k)
        ).wait_recv()

    def select(j, carry):
        slot, found = 0, 0.0
        for k in range(blocks):
            hit = codes_ref[lax.rem(block + blocks - k, blocks), 0] == j
            slot = jnp.where(hit, k, slot)
            found = jnp.where(hit, 1.0, found)
        total = pooled_got[slot].astype(F32) * found
        pooled_sel[lax.div(j, work), lax.rem(j, work)] = total.astype(BF16)
        return carry

    lax.fori_loop(0, regions * work, select, 0)
    for k in range(1, regions):
        peer = lax.rem(region + k, regions)
        start(pooled_sel.at[peer], pooled_end.at[k], q_send.at[k], q_recv.at[k], along(k))
    bias_sum = bias_ref[...]
    for k in range(1, blocks):
        remote(bias_ref, bias_got.at[k], b_send.at[k], b_recv.at[k], across(k)).wait_recv()
        bias_sum = bias_sum + bias_got[k]
    bias_part[region] = bias_sum
    for k in range(1, regions):
        start(
            bias_part.at[region], bias_part.at[region], c_send.at[k], c_recv.at[k], along(k)
        )

    for j in range(1, chips):
        remote(
            pair_sum.at[j], grad_got.at[j], g_send.at[j], g_recv.at[j], other_chip(j)
        ).wait_recv()
        grad_sum = grad_sum + grad_got[j].astype(F32)
    grad_part[...] = grad_sum.reshape(grad_part.shape)
    for k in range(1, regions):
        peer = lax.rem(region + k, regions)
        start(grad_part.at[peer], grad_slice.at[k], h_send.at[k], h_recv.at[k], along(k))
    for k in range(1, regions):
        remote(
            grad_part.at[0], grad_slice.at[k], h_send.at[k], h_recv.at[k], along(k)
        ).wait_recv()
    grad_sum = grad_part[region]
    for k in range(1, regions):
        grad_sum = grad_sum + grad_slice[k]
    grad_full[region] = grad_sum
    for k in range(1, regions):
        start(
            grad_full.at[region], grad_full.at[region], d_send.at[k], d_recv.at[k], along(k)
        )
    for k in range(1, regions):
        source = lax.rem(region + regions - k, regions)
        remote(
            grad_full.at[source], grad_full.at[source], d_send.at[k], d_recv.at[k], along(k)
        ).wait_recv()
    grad_sum = grad_full[...].reshape(shard, -1)
    own = grad_all.at[core, chip]
    own[...] = grad_sum.astype(BF16)
    for j in range(1, chips):
        start(own, own, a_send.at[j], a_recv.at[j], other_chip(j))
    start(own, own, f_send.at[0], f_recv.at[0], sibling)
    for j in range(1, chips):
        slot = grad_all.at[core, lax.rem(chip + chips - j, chips)]
        remote(slot, slot, a_send.at[j], a_recv.at[j], other_chip(j)).wait_recv()
        start(slot, slot, f_send.at[j], f_recv.at[j], sibling)

    for k in range(1, regions):
        source = lax.rem(region + regions - k, regions)
        remote(
            bias_part.at[source], bias_part.at[source], c_send.at[k], c_recv.at[k], along(k)
        ).wait_recv()
        remote(
            pooled_sel.at[0], pooled_end.at[k], q_send.at[k], q_recv.at[k], along(k)
        ).wait_recv()
    bias_sum = bias_part[0]
    for r in range(1, regions):
        bias_sum = bias_sum + bias_part[r]
    bias_out[...] = bias_sum[:1]
    for s in range(work):
        rows = pooled_sel[region, s].astype(F32)
        for k in range(1, regions):
            rows = rows + pooled_end[k, s].astype(F32)
        width = rows.shape[1] // 2
        pooled_ref[s] = jnp.concatenate([rows[:, :width], rows[:, width:]], axis=0).astype(BF16)

    for j in range(chips):
        slot = grad_all.at[1 - core, lax.rem(chip + chips - j, chips)]
        remote(slot, slot, f_send.at[j], f_recv.at[j], sibling).wait_recv()
    rows_total = weight_out.shape[0]
    for w in range(blocks):
        low, high = w * shard, min((w + 1) * shard, rows_total)
        if low < high:
            weight_out[low:high, :] = grad_all[w // chips, w % chips, : high - low, :].astype(F32)
    for copy in sends:
        copy.wait_send()


def per_device(
    features,
    counts,
    rebalance,
    neighbors,
    coarse_owner,
    conv_weight,
    convolution_bias_vector,
    merged_adjoint,
):
    home, channels = features.shape[0], features.shape[1]
    taps, _, outs = conv_weight.shape
    work = home // 2
    regions, blocks = lax.axis_size("region"), lax.axis_size("block")
    cells = merged_adjoint.shape[1] // outs
    rows = taps * channels
    dense = (outs // 2, 2 * cells)
    chips = blocks // 2
    unit = math.lcm(16, 8 * regions)
    shard = -(-rows // (blocks * unit)) * unit
    vmem = pl.BlockSpec(memory_space=pltpu.VMEM)
    smem = pl.BlockSpec(memory_space=pltpu.SMEM)
    dma = pltpu.SemaphoreType.DMA
    shape = jax.ShapeDtypeStruct

    pooled, weight_total, bias_total = pl.pallas_call(
        functools.partial(fused_kernel, regions, blocks, shard),
        out_shape=(
            shape((work, outs, cells), BF16),
            shape((rows, outs), F32),
            shape((1, outs), F32),
        ),
        in_specs=[smem] * 4 + [vmem] * 4,
        out_specs=(vmem, vmem, vmem),
        scratch_shapes=[
            pltpu.VMEM((3, home, channels, 128), BF16),
            pltpu.VMEM((blocks,) + dense, BF16),
            pltpu.VMEM((blocks, 128), jnp.int32),
            pltpu.VMEM((blocks, blocks, 128), jnp.int32),
            pltpu.SMEM((blocks, 128), jnp.int32),
            pltpu.VMEM((regions * work,) + dense, BF16),
            pltpu.VMEM((blocks,) + dense, BF16),
            pltpu.VMEM((home + 1, channels, 512), F32),
            pltpu.VMEM((3 * home + 1, channels, 128), F32),
            pltpu.VMEM((home, rows, 512), BF16),
            pltpu.VMEM((home, outs, 512), F32),
            pltpu.VMEM((home,) + dense, BF16),
            pltpu.VMEM((blocks,) + dense, BF16),
            pltpu.VMEM((blocks * shard, outs), F32),
            pltpu.VMEM((8, outs), F32),
            pltpu.VMEM((blocks,) + dense, BF16),
            pltpu.VMEM((regions, work) + dense, BF16),
            pltpu.VMEM((regions, work) + dense, BF16),
            pltpu.VMEM((chips, shard, outs), F32),
            pltpu.VMEM((chips, shard, outs), BF16),
            pltpu.VMEM((chips, shard, outs), BF16),
            pltpu.VMEM((regions, shard // regions, outs), F32),
            pltpu.VMEM((regions, shard // regions, outs), F32),
            pltpu.VMEM((regions, shard // regions, outs), F32),
            pltpu.VMEM((2, chips, shard, outs), BF16),
            pltpu.VMEM((blocks, 8, outs), F32),
            pltpu.VMEM((regions, 8, outs), F32),
            dma,
            dma((2,)),
            dma((2,)),
        ]
        + [dma((regions,))] * 10
        + [dma((blocks,))] * 8
        + [dma((chips,))] * 8,
        compiler_params=pltpu.CompilerParams(
            collective_id=0, has_side_effects=True, vmem_limit_bytes=VMEM_LIMIT
        ),
        name="fused",
    )(
        counts,
        rebalance,
        coarse_owner,
        neighbors,
        features,
        merged_adjoint.reshape(work, outs, cells),
        conv_weight.reshape(rows, outs),
        convolution_bias_vector.reshape(1, outs),
    )
    return (
        pooled.reshape(work, outs * cells),
        weight_total.reshape(taps, channels, outs),
        bias_total.reshape(outs),
    )


def solution(mesh):
    in_specs = (
        P(("region", "block"), None, None),
        P(("region", "block")),
        P(("region", "block")),
        P(("region", "block"), None),
        P(("region", "block")),
        P(),
        P(),
        P(("region", "block"), None),
    )
    out_specs = (P(("region", "block"), None), P(), P())
    return jax.shard_map(
        per_device, mesh=mesh, in_specs=in_specs, out_specs=out_specs, check_vma=False
    )
```
